512 devices in a mesh: rows: 128 (over z, y, core), ingest: 4 (over x).
Axes of the slice: x: 4, y: 8, z: 8, core: 2. Of those that a mesh axis runs over, the one named last changes fastest.
Arguments:
- covariates: float32 [64, 4194304], P(None, ('rows', 'ingest')), may hold values from -6 to 6
- intervals: int32 [4194304], P(('rows', 'ingest')), may hold values from 0 to 4
- offsets: float32 [4194304], P(('rows', 'ingest')), may hold values from 0 to 1
- responses: float32 [4194304], P(('rows', 'ingest')), may hold values from -6 to 6
- counts: int32 [512], P(('rows', 'ingest')), may hold values from 1 to 8192, 2097152 in all
- smoothing: float32 [64], replicated, may hold values from 0.01 to 1
Outputs:
- factor: float32 [512, 512], replicated
- projected: float32 [512], replicated
The draws below stay inside these ranges and needn't reach their ends.
Inputs may be any that keep to these rules, and one draw needn't show every extreme that they name: A device's live rows are its first counts slots; the counts sum to 2097152 and one device is full.
All inputs are finite; a program needn't handle non-finite values.
Results may differ from the reference program's by a relative error of at most 0.0003.
Values sent between devices are 32-bit elements; how exact they have to be, the bound alone decides.
No kernel may reach another device: no remote copies, remote signals or barrier semaphores. Data moves between devices by JAX's collectives and lax.ppermute only.
A program may use at most 128 MiB of HBM per device.

```python
import math
import jax
import jax.numpy as jnp
import numpy as np
from jax import lax

P_COV = 64
N_BASIS = 8
COLS = 512
CAP = 8192
ROWS_ALL = 4194304
TOTAL_LIVE = 2097152
DEVICES = 512


def place_ends(entries, stream_key, low, high):
    extent = entries.shape
    spot = [jax.random.randint(jax.random.fold_in(stream_key, axis), (), 0, extent[axis]) for axis in range(len(extent))]
    entries = entries.at[tuple(spot)].set(low)
    longest = extent.index(max(extent))
    spot[longest] = (spot[longest] + 1) % extent[longest]
    return entries.at[tuple(spot)].set(high)


def level_of(key, shape, split, smallest, top_value):
    level = 1.0
    for axis_at, blocks in split:
        heights = jax.random.uniform(jax.random.fold_in(jax.random.fold_in(key, 6), axis_at), (blocks,), jnp.float32, smallest / len(split), top_value / len(split))
        level = level * jnp.repeat(jnp.exp(heights), shape[axis_at] // blocks).reshape((-1,) + (1,) * (len(shape) - 1 - axis_at))
    return level


def profile(number_of, total, bound, slope):
    weights = [(1 << 20) // math.isqrt(grade ** slope) + 1 for grade in range(2, number_of + 1)]
    rest, given = total - bound - (number_of - 1), [1] * (number_of - 1)
    while rest > 0:
        candidates = [i for i in range(number_of - 1) if given[i] < bound]
        pool, left = sum([weights[i] for i in candidates]), rest
        for i in candidates:
            addition = min(bound - given[i], max(1, left * weights[i] // pool), rest)
            given[i] = given[i] + addition
            rest = rest - addition
    return np.array([bound] + given)


def uneven(key, count, total, bound, slope):
    if count == 2:
        one = jax.random.randint(key, (), max(1, total - bound), min(bound, total - 1) + 1)
        return jnp.stack([one, total - one])
    sizes = jnp.asarray(profile(count, total, bound, slope), jnp.int32)
    pairs = (count - 1) // 2
    source_of, sink = sizes[1:1 + 2 * pairs:2], sizes[2:2 + 2 * pairs:2]
    slack = jnp.minimum(source_of - 1, bound - sink)
    shifted = jax.random.randint(jax.random.fold_in(key, 1), (pairs,), 0, 1 << 20) % (slack + 1)
    sizes = sizes.at[1:1 + 2 * pairs:2].set(source_of - shifted).at[2:2 + 2 * pairs:2].set(sink + shifted)
    return sizes[jax.random.permutation(jax.random.fold_in(key, 2), count)]


def scatter_about(rng, shape, scale, reach, split=(), kind=jnp.bfloat16):
    gain = level_of(rng, shape, split, -0.22, 0.18) if split else 1.0
    entries = jax.random.normal(rng, shape, jnp.float32) * scale * gain
    return jnp.minimum(jnp.maximum(entries, -reach), reach).astype(kind)


def setup_inputs(seed: int = 0) -> dict:
    key_of = jax.random.split(jax.random.key(seed), 7)
    return {
        "covariates": scatter_about(key_of[0], (P_COV, ROWS_ALL), 1.0, 6.0, ((1, 512),), jnp.float32),
        "intervals": place_ends(jax.random.randint(key_of[1], (ROWS_ALL,), 0, N_BASIS - 3), jax.random.fold_in(key_of[1], 1), 0, (N_BASIS - 3) - 1).astype(jnp.int32),
        "offsets": jnp.clip(1.0 * jax.random.uniform(key_of[2], (ROWS_ALL,), jnp.float32) ** level_of(key_of[2], (ROWS_ALL,), ((0, 512),), -0.2, 0.2), 0.0, 1.0),
        "responses": scatter_about(key_of[3], (ROWS_ALL,), 1.0, 6.0, ((0, 512),), jnp.float32),
        "counts": uneven(key_of[4], DEVICES, TOTAL_LIVE, CAP, 2).astype(jnp.int32),
        "smoothing": jnp.clip(jnp.exp(jax.random.uniform(key_of[5], (P_COV,), jnp.float32, math.log(0.01), math.log(1.0))), 0.01, 1.0),
    }


def spline_values(intervals, offsets):
    within = offsets
    first = (1.0 - within) ** 3 / 6.0
    second = (3.0 * within ** 3 - 6.0 * within ** 2 + 4.0) / 6.0
    third = (-3.0 * within ** 3 + 3.0 * within ** 2 + 3.0 * within + 1.0) / 6.0
    fourth = within ** 3 / 6.0
    basis_ids = jnp.arange(N_BASIS, dtype=jnp.int32)[:, None]
    result = jnp.where(intervals[None, :] == basis_ids, first[None, :], 0.0)
    result = result + jnp.where(intervals[None, :] + 1 == basis_ids, second[None, :], 0.0)
    result = result + jnp.where(intervals[None, :] + 2 == basis_ids, third[None, :], 0.0)
    result = result + jnp.where(intervals[None, :] + 3 == basis_ids, fourth[None, :], 0.0)
    return result

def penalty(smoothing):
    identity = jnp.eye(N_BASIS, dtype=jnp.float32)
    second = identity[:-2] - 2.0 * identity[1:-1] + identity[2:]
    kernel = jnp.dot(second.T.astype(jnp.float32), second.astype(jnp.float32), precision=lax.Precision.HIGHEST, preferred_element_type=jnp.float32)
    same_cov = jnp.eye(P_COV, dtype=jnp.float32)
    blocks = same_cov[:, None, :, None] * smoothing[:, None, None, None] * kernel[None, :, None, :]
    return blocks.reshape(COLS, COLS)

def reference(covariates, intervals, offsets, responses, counts, smoothing):
    cov_blocks = covariates.reshape(P_COV, DEVICES, CAP).transpose(1, 0, 2)
    int_blocks = intervals.reshape(DEVICES, CAP)
    off_blocks = offsets.reshape(DEVICES, CAP)
    resp_blocks = responses.reshape(DEVICES, CAP)

    def device_step(state_pair, inputs):
        cov_block, int_block, off_block, resp_block, live_count = inputs
        basis = spline_values(int_block, off_block)
        live_mask = (jnp.arange(CAP, dtype=jnp.int32) < live_count).astype(jnp.float32)
        design = (cov_block[:, None, :] * basis[None, :, :]).reshape(COLS, CAP) * live_mask[None, :]
        gram_part = lax.dot_general(design.astype(jnp.float32), design.astype(jnp.float32), (((1,), (1,)), ((), ())), precision=lax.Precision.HIGHEST, preferred_element_type=jnp.float32)
        moment_part = jnp.dot(design.astype(jnp.float32), resp_block.astype(jnp.float32), precision=lax.Precision.HIGHEST, preferred_element_type=jnp.float32)
        return ((state_pair[0] + gram_part, state_pair[1] + moment_part), None)
    start_pair = (jnp.zeros((COLS, COLS), jnp.float32), jnp.zeros((COLS,), jnp.float32))
    (gram_matrix, moment), _ = lax.scan(device_step, start_pair, (cov_blocks, int_blocks, off_blocks, resp_blocks, counts))
    gram_matrix = gram_matrix / TOTAL_LIVE + penalty(smoothing)
    moment = moment / jnp.sqrt(jnp.float32(TOTAL_LIVE))
    lower_factor = jnp.linalg.cholesky(gram_matrix)
    projected = lax.linalg.triangular_solve(lower_factor, moment[:, None], left_side=True, lower=True)[:, 0]
    return (lower_factor.T, projected)
```

```python
import math

import jax
import jax.numpy as jnp
import numpy as np
from jax import lax
from jax.experimental import pallas as pl
from jax.experimental.pallas import tpu as pltpu
from jax.sharding import Mesh, PartitionSpec as P

P_COV = 64
N_BASIS = 8
WIDTH = P_COV * N_BASIS
CHUNK = 2048
TOTAL_LIVE = 2097152
F32 = jnp.float32
BF16 = jnp.bfloat16
HIGHEST = lax.Precision.HIGHEST

PAIRS = [(j, k) for j in range(4) for k in range(j + 1)]
PAIRS += [(j, k) for j in range(4, 7) for k in range(1, 4) if j - k <= 3]
PAIRS += [(j, k) for j in range(4, 8) for k in range(4, j + 1)]
HALF = len(PAIRS) // 2
SHARES = 32
SHARE_ROWS = 16
SLAB_ROWS = SHARES * SHARE_ROWS
DIAG_ROW = 448
MOMENT_ROW = 464
NT = (((1,), (1,)), ((), ()))
TN = (((0,), (0,)), ((), ()))


def slab_place(pair_index):
    return (pair_index // 2) * P_COV, (pair_index % 2) * P_COV


def gram_kernel(count_ref, cov_ref, int_ref, off_ref, resp_ref, out_ref, hi_ref, lo_ref, hh_ref, lh_ref, mom_ref):
    step = pl.program_id(0)
    count = count_ref[0]

    @pl.when(step == 0)
    def _():
        hh_ref[...] = jnp.zeros_like(hh_ref)
        lh_ref[...] = jnp.zeros_like(lh_ref)
        mom_ref[...] = jnp.zeros_like(mom_ref)

    @pl.when(step * CHUNK < count)
    def _():
        cov = cov_ref[...]
        interval = int_ref[...]
        within = off_ref[...]
        slot = lax.broadcasted_iota(jnp.int32, (1, CHUNK), 1) + step * CHUNK
        live = jnp.where(slot < count, 1.0, 0.0).astype(F32)
        square = within * within
        cube = square * within
        rest = 1.0 - within
        first = rest * rest * rest * (1.0 / 6.0) * live
        second = (3.0 * cube - 6.0 * square + 4.0) * (1.0 / 6.0) * live
        third = (-3.0 * cube + 3.0 * square + 3.0 * within + 1.0) * (1.0 / 6.0) * live
        fourth = cube * (1.0 / 6.0) * live
        weights = []
        for j in range(N_BASIS):
            value = jnp.where(interval == j, first, 0.0)
            value = jnp.where(interval + 1 == j, second, value)
            value = jnp.where(interval + 2 == j, third, value)
            value = jnp.where(interval + 3 == j, fourth, value)
            weights.append(value)
            design = cov * value
            high = design.astype(BF16)
            hi_ref[j * P_COV : (j + 1) * P_COV, :] = high
            lo_ref[j * P_COV : (j + 1) * P_COV, :] = (design - high.astype(F32)).astype(BF16)
        cov_high = cov.astype(BF16)
        cov_low = (cov - cov_high.astype(F32)).astype(BF16)
        weighted = jnp.concatenate(weights, axis=0) * resp_ref[...]
        weighted_high = weighted.astype(BF16)
        weighted_low = (weighted - weighted_high.astype(F32)).astype(BF16)
        mom_ref[...] += lax.dot_general(
            jnp.concatenate([weighted_high, weighted_low], axis=0),
            jnp.concatenate([cov_high, cov_low], axis=0),
            NT,
            preferred_element_type=F32,
        )

        def product(left_ref, rows, columns):
            return lax.dot_general(left_ref[rows, :], hi_ref[columns, :], NT, preferred_element_type=F32)

        low, high_half = slice(0, 256), slice(256, 512)
        hh_ref[0:448, low] += product(hi_ref, slice(0, 448), low)
        lh_ref[0:448, low] += product(lo_ref, slice(0, 448), low)
        hh_ref[high_half, high_half] += product(hi_ref, high_half, high_half)
        lh_ref[64:512, high_half] += product(lo_ref, slice(64, 512), high_half)

    @pl.when(step == pl.num_programs(0) - 1)
    def _():
        row = lax.broadcasted_iota(jnp.int32, (P_COV, P_COV), 0)
        column = lax.broadcasted_iota(jnp.int32, (P_COV, P_COV), 1)

        def block(ref, j, k):
            return ref[j * P_COV : (j + 1) * P_COV, k * P_COV : (k + 1) * P_COV]

        def full(pair):
            j, k = pair
            return block(hh_ref, j, k) + block(lh_ref, j, k) + block(lh_ref, k, j).T

        out_ref[DIAG_ROW - 64 :, :] = jnp.zeros((SLAB_ROWS - DIAG_ROW + 64, 128), F32)
        for i in range(HALF):
            upper, lower = full(PAIRS[i]), full(PAIRS[HALF + i])
            r0, c0 = slab_place(i)
            out_ref[r0 : r0 + P_COV, c0 : c0 + P_COV] = jnp.where(row <= column, upper, lower)
            out_ref[DIAG_ROW + i : DIAG_ROW + i + 1, 0:P_COV] = jnp.sum(
                jnp.where(row == column, lower, 0.0), axis=0, keepdims=True
            )
        mom = mom_ref[...]
        out_ref[MOMENT_ROW : MOMENT_ROW + N_BASIS, 0:P_COV] = (
            mom[0:8, 0:P_COV] + mom[8:16, 0:P_COV] + mom[0:8, P_COV:]
        )


def local_sums(count, covariates, intervals, offsets, responses):
    slots = covariates.shape[1]
    per_row = pl.BlockSpec((1, CHUNK), lambda i: (0, i))
    return pl.pallas_call(
        gram_kernel,
        grid=(slots // CHUNK,),
        in_specs=[
            pl.BlockSpec(memory_space=pltpu.SMEM),
            pl.BlockSpec((P_COV, CHUNK), lambda i: (0, i)),
            per_row,
            per_row,
            per_row,
        ],
        out_specs=pl.BlockSpec((SLAB_ROWS, 128), lambda i: (0, 0)),
        out_shape=jax.ShapeDtypeStruct((SLAB_ROWS, 128), F32),
        scratch_shapes=[
            pltpu.VMEM((WIDTH, CHUNK), BF16),
            pltpu.VMEM((WIDTH, CHUNK), BF16),
            pltpu.VMEM((WIDTH, WIDTH), F32),
            pltpu.VMEM((WIDTH, WIDTH), F32),
            pltpu.VMEM((16, 128), F32),
        ],
        compiler_params=pltpu.CompilerParams(
            dimension_semantics=("arbitrary",), vmem_limit_bytes=40 * 1024 * 1024
        ),
        name="local_sums",
    )(count, covariates, intervals[None, :], offsets[None, :], responses[None, :])


def sum_repeat_kernel(parts, copies, in_ref, out_ref):
    rows = in_ref.shape[0] // parts
    total = in_ref[0:rows, :]
    for i in range(1, parts):
        total = total + in_ref[i * rows : (i + 1) * rows, :]
    for i in range(copies):
        out_ref[i * rows : (i + 1) * rows, :] = total


def sum_repeat(received, parts, copies):
    rows = received.shape[0] // parts
    return pl.pallas_call(
        lambda a, b: sum_repeat_kernel(parts, copies, a, b),
        out_shape=jax.ShapeDtypeStruct((copies * rows, 128), F32),
        name="sum_repeat",
    )(received)


def lane_spread(tile, lane):
    return jnp.broadcast_to(tile[:, lane : lane + 1], tile.shape)


def row_spread(tile, row):
    return jnp.broadcast_to(tile[row : row + 1, :], tile.shape)


def factor_tile(work, side):
    blocks = len(work)
    lanes = lax.broadcasted_iota(jnp.int32, (8, 128), 1)
    subs = lax.broadcasted_iota(jnp.int32, (8, 128), 0)
    factor_rows, inverse_rows = [], []
    for k in range(blocks):
        columns = [lane_spread(work[k], 8 * k + t) for t in range(8)]
        entry = {(s, t): row_spread(columns[t], s) for t in range(8) for s in range(t, 8)}
        rows = [row_spread(work[k], t) for t in range(8)]
        siderows = [row_spread(side[k], t) for t in range(8)]
        reciprocals, scale = [], {}
        for t in range(8):
            reciprocals.append(1.0 / entry[t, t])
            for s in range(t + 1, 8):
                scale[s, t] = entry[s, t] * reciprocals[t]
            for s in range(t + 1, 8):
                for u in range(t + 1, s + 1):
                    entry[s, u] = entry[s, u] - scale[s, t] * entry[u, t]
                rows[s] = rows[s] - scale[s, t] * rows[t]
                siderows[s] = siderows[s] - scale[s, t] * siderows[t]
        for b in range(k + 1, blocks):
            c = [lane_spread(work[b], 8 * k + t) for t in range(8)]
            for t in range(8):
                for s in range(t + 1, 8):
                    c[s] = c[s] - scale[s, t] * c[t]
                weight = c[t] * reciprocals[t]
                work[b] = work[b] - weight * rows[t]
                side[b] = side[b] - weight * siderows[t]
        out, sideout = jnp.zeros((8, 128), F32), jnp.zeros((8, 128), F32)
        for t in range(8):
            root = lax.rsqrt(entry[t, t])
            out = jnp.where(subs == t, rows[t] * root, out)
            sideout = jnp.where(subs == t, siderows[t] * root, sideout)
        factor_rows.append(jnp.where(lanes >= subs + 8 * k, out, 0.0))
        inverse_rows.append(jnp.where(lanes <= subs + 8 * k, sideout, 0.0))
    return factor_rows, inverse_rows


def factor_kernel(sums_ref, smooth_ref, factor_ref, proj_ref, half_ref, gram_ref, inv_ref):
    row = lax.broadcasted_iota(jnp.int32, (P_COV, P_COV), 0)
    column = lax.broadcasted_iota(jnp.int32, (P_COV, P_COV), 1)
    second = np.zeros((N_BASIS - 2, N_BASIS))
    for i in range(N_BASIS - 2):
        second[i, i : i + 3] = (1.0, -2.0, 1.0)
    penalty = second.T @ second
    smooth = jnp.where(row == column, smooth_ref[...], 0.0)
    pieces = {}

    def put(pair, value):
        j, k = pair
        value = value * (1.0 / TOTAL_LIVE)
        if penalty[j, k]:
            value = value + smooth * float(penalty[j, k])
        pieces[j, k] = pieces[k, j] = value

    for i in range(HALF):
        r0, c0 = slab_place(i)
        packed = sums_ref[r0 : r0 + P_COV, c0 : c0 + P_COV]
        turned = packed.T
        put(PAIRS[i], jnp.where(row <= column, packed, turned))
        diagonal = jnp.broadcast_to(sums_ref[DIAG_ROW + i : DIAG_ROW + i + 1, 0:P_COV], (P_COV, P_COV))
        lower = jnp.where(row > column, packed, turned)
        put(PAIRS[HALF + i], jnp.where(row == column, diagonal, lower))
    nothing = jnp.zeros((P_COV, P_COV), F32)
    for j in range(N_BASIS):
        for w in range(4):
            half_ref[w, pl.ds(j, P_COV, N_BASIS), :] = jnp.concatenate(
                [pieces.get((j, 2 * w), nothing), pieces.get((j, 2 * w + 1), nothing)], axis=1
            )
    for w in range(4):
        for i in range(4):
            turned = half_ref[w, 128 * i : 128 * i + 128, :].T
            for k in (2 * w, 2 * w + 1):
                gram_ref[i, pl.ds(k, P_COV, N_BASIS), :] = turned[(k - 2 * w) * P_COV : (k - 2 * w + 1) * P_COV, :]
    moment = sums_ref[MOMENT_ROW : MOMENT_ROW + N_BASIS, 0:P_COV].T * (1.0 / math.sqrt(TOTAL_LIVE))
    for j in range(N_BASIS):
        gram_ref[4, pl.ds(j, P_COV, N_BASIS), :] = jnp.broadcast_to(moment[:, j : j + 1], (P_COV, 128))

    factor_ref[...] = jnp.zeros_like(factor_ref)
    lanes = lax.broadcasted_iota(jnp.int32, (8, 128), 1)
    subs = lax.broadcasted_iota(jnp.int32, (8, 128), 0)

    def panel(p, _):
        start = pl.multiple_of(p * 128, 128)
        work = [gram_ref[p, pl.ds(pl.multiple_of(start + 8 * b, 8), 8), :] for b in range(16)]
        side = [jnp.where(lanes == subs + 8 * b, 1.0, 0.0).astype(F32) for b in range(16)]
        factor_rows, inverse_rows = factor_tile(work, side)
        for b in range(16):
            inv_ref[8 * b : 8 * b + 8, :] = inverse_rows[b]
            factor_ref[pl.ds(pl.multiple_of(start + 8 * b, 8), 8), pl.ds(start, 128)] = factor_rows[b]

        for q in range(4):

            @pl.when(p == q)
            def _():
                mine = slice(128 * q, 128 * q + 128)
                inverse = inv_ref[...]
                solved = {}
                for w in range(q + 1, 5):
                    solved[w] = jnp.dot(inverse, gram_ref[w, mine, :], precision=HIGHEST, preferred_element_type=F32)
                    gram_ref[w, mine, :] = solved[w]
                    if w < 4:
                        factor_ref[mine, 128 * w : 128 * w + 128] = solved[w]
                for i in range(q + 1, 4):
                    for w in range(i, 5):
                        gram_ref[w, 128 * i : 128 * i + 128, :] -= lax.dot_general(
                            solved[i], solved[w], TN, precision=HIGHEST, preferred_element_type=F32
                        )

        return 0

    lax.fori_loop(0, 4, panel, 0)
    diagonal_mask = lax.broadcasted_iota(jnp.int32, (128, 128), 0) == lax.broadcasted_iota(jnp.int32, (128, 128), 1)
    for p in range(4):
        tile = gram_ref[4, 128 * p : 128 * p + 128, :]
        proj_ref[:, 128 * p : 128 * p + 128] = jnp.sum(jnp.where(diagonal_mask, tile, 0.0), axis=0, keepdims=True)


def factorize(sums, smoothing):
    return pl.pallas_call(
        factor_kernel,
        out_shape=(
            jax.ShapeDtypeStruct((WIDTH, WIDTH), F32),
            jax.ShapeDtypeStruct((1, WIDTH), F32),
        ),
        scratch_shapes=[
            pltpu.VMEM((4, WIDTH, 128), F32),
            pltpu.VMEM((5, WIDTH, 128), F32),
            pltpu.VMEM((128, 128), F32),
        ],
        compiler_params=pltpu.CompilerParams(vmem_limit_bytes=40 * 1024 * 1024),
        name="factorize",
    )(sums, smoothing[None, :])


def per_device(covariates, intervals, offsets, responses, counts, smoothing):
    sums = local_sums(counts, covariates, intervals, offsets, responses)
    received = lax.all_to_all(sums.reshape(32, 16, 128), ("z", "x"), 0, 0, tiled=True)
    spread = sum_repeat(received.reshape(512, 128), 32, 16)
    received = lax.all_to_all(spread.reshape(16, 16, 128), ("y", "c"), 0, 0, tiled=True)
    spread = sum_repeat(received.reshape(256, 128), 16, 32)
    sums = lax.all_to_all(spread.reshape(32, 16, 128), ("z", "x"), 0, 0, tiled=True)
    factor, projected = factorize(sums.reshape(512, 128), smoothing)
    return factor, projected[0]


def solution(mesh):
    fine = Mesh(mesh.devices.reshape(8, 8, 2, 4), ("z", "y", "c", "x"))
    spread = ("z", "y", "c", "x")
    return jax.shard_map(
        per_device,
        mesh=fine,
        in_specs=(P(None, spread), P(spread), P(spread), P(spread), P(spread), P()),
        out_specs=(P(), P()),
        check_vma=False,
    )
```

```python
import math

import jax
import jax.numpy as jnp
import numpy as np
from jax import lax
from jax.experimental import pallas as pl
from jax.experimental.pallas import tpu as pltpu
from jax.sharding import Mesh, PartitionSpec as P

P_COV = 64
N_BASIS = 8
WIDTH = P_COV * N_BASIS
CHUNK = 1024
TOTAL_LIVE = 2097152
F32 = jnp.float32
BF16 = jnp.bfloat16
HIGHEST = lax.Precision.HIGHEST

ROW_SLABS = [(0, 0, 4), (0, 1, 1), (0, 2, 2), (0, 3, 3), (1, 2, 6), (1, 3, 3), (1, 4, 4), (1, 5, 5)]
ROW_SLABS += [(2, 4, 4), (2, 5, 5), (2, 6, 6), (2, 7, 7), (3, 6, 6), (3, 7, 7)]
HALF = len(ROW_SLABS) // 2
SHARES = 32
SHARE_ROWS = 16
SLAB_ROWS = SHARES * SHARE_ROWS
DIAG_ROW = HALF * P_COV
MOMENT_ROW = DIAG_ROW + 8
NT = (((1,), (1,)), ((), ()))
TN = (((0,), (0,)), ((), ()))


def slab_masks():
    row = lax.broadcasted_iota(jnp.int32, (P_COV, 128), 0)
    column = lax.broadcasted_iota(jnp.int32, (P_COV, 128), 1)
    return row, column % P_COV, column < P_COV


def gram_kernel(
    count_ref, cov_hbm, int_hbm, off_hbm, resp_hbm, out_ref,
    cov_ref, int_ref, off_ref, resp_ref, hi_even, hi_odd, lo_even, lo_odd, hh_ref, lh_ref, mom_ref, row_sem, cov_sem,
):
    count = count_ref[0]
    chunks = cov_hbm.shape[1] // CHUNK

    def columns(c):
        return pl.ds(pl.multiple_of(c * CHUNK, CHUNK), CHUNK)

    row_copies = [
        pltpu.make_async_copy(source, target, row_sem.at[i])
        for i, (source, target) in enumerate([(int_hbm, int_ref), (off_hbm, off_ref), (resp_hbm, resp_ref)])
    ]
    cov_copies = [
        pltpu.make_async_copy(cov_hbm.at[:, part], cov_ref.at[:, part], cov_sem.at[i])
        for i, part in enumerate([slice(0, CHUNK), slice(CHUNK, chunks * CHUNK)])
    ]
    for copy in [*row_copies, *cov_copies]:
        copy.start()
    hh_ref[...] = jnp.zeros_like(hh_ref)
    lh_ref[...] = jnp.zeros_like(lh_ref)
    mom_ref[...] = jnp.zeros_like(mom_ref)
    for copy in row_copies:
        copy.wait()

    def build(c, hi_ref, lo_ref):
        part = columns(jnp.minimum(c, chunks - 1))
        cov = cov_ref[:, part]
        interval = int_ref[:, part]
        within = off_ref[:, part]
        slot = lax.broadcasted_iota(jnp.int32, (1, CHUNK), 1) + c * CHUNK
        live = jnp.where(slot < count, 1.0, 0.0).astype(F32)
        square = within * within
        cube = square * within
        rest = 1.0 - within
        first = rest * rest * rest * (1.0 / 6.0) * live
        second = (3.0 * cube - 6.0 * square + 4.0) * (1.0 / 6.0) * live
        third = (-3.0 * cube + 3.0 * square + 3.0 * within + 1.0) * (1.0 / 6.0) * live
        fourth = cube * (1.0 / 6.0) * live
        weights = []
        for j in range(N_BASIS):
            value = jnp.where(interval == j, first, 0.0)
            value = jnp.where(interval + 1 == j, second, value)
            value = jnp.where(interval + 2 == j, third, value)
            value = jnp.where(interval + 3 == j, fourth, value)
            weights.append(value)
            design = cov * value
            high = design.astype(BF16)
            hi_ref[j * P_COV : (j + 1) * P_COV, :] = high
            lo_ref[j * P_COV : (j + 1) * P_COV, :] = (design - high.astype(F32)).astype(BF16)
        cov_high = cov.astype(BF16)
        cov_low = (cov - cov_high.astype(F32)).astype(BF16)
        weighted = jnp.concatenate(weights, axis=0) * resp_ref[:, part]
        weighted_high = weighted.astype(BF16)
        weighted_low = (weighted - weighted_high.astype(F32)).astype(BF16)
        mom_ref[...] += lax.dot_general(
            jnp.concatenate([weighted_high, weighted_low], axis=0),
            jnp.concatenate([cov_high, cov_low], axis=0),
            NT,
            preferred_element_type=F32,
        )

    def multiply(hi_ref, lo_ref):
        def product(left_ref, rows, columns):
            return lax.dot_general(left_ref[rows, :], hi_ref[columns, :], NT, preferred_element_type=F32)

        low, high_half = slice(0, 256), slice(256, 512)
        hh_ref[0:448, low] += product(hi_ref, slice(0, 448), low)
        lh_ref[0:448, low] += product(lo_ref, slice(0, 448), low)
        hh_ref[high_half, high_half] += product(hi_ref, high_half, high_half)
        lh_ref[64:512, high_half] += product(lo_ref, slice(64, 512), high_half)

    cov_copies[0].wait()
    build(0, hi_even, lo_even)
    cov_copies[1].wait()

    def pair(i, _):
        build(2 * i + 1, hi_odd, lo_odd)
        multiply(hi_even, lo_even)
        build(2 * i + 2, hi_even, lo_even)
        multiply(hi_odd, lo_odd)
        return 0

    lax.fori_loop(0, pl.cdiv(count, 2 * CHUNK), pair, 0)

    row, column, left = slab_masks()
    tiles = {}

    def row_slab(entry):
        w, j_left, j_right = entry
        pieces = []
        for j in (j_left, j_right):
            t = j // 2
            if (t, w) not in tiles:
                at, across = slice(128 * t, 128 * t + 128), slice(128 * w, 128 * w + 128)
                tiles[t, w] = hh_ref[at, across] + lh_ref[at, across] + lh_ref[across, at].T
            pieces.append(tiles[t, w][(j % 2) * P_COV : (j % 2 + 1) * P_COV, :])
        return pieces[0] if j_left == j_right else jnp.where(left, pieces[0], pieces[1])

    out_ref[DIAG_ROW:, :] = jnp.zeros((SLAB_ROWS - DIAG_ROW, 128), F32)
    for i in range(HALF):
        upper, lower = row_slab(ROW_SLABS[i]), row_slab(ROW_SLABS[HALF + i])
        out_ref[i * P_COV : (i + 1) * P_COV, :] = jnp.where(row <= column, upper, lower)
        out_ref[DIAG_ROW + i : DIAG_ROW + i + 1, :] = jnp.sum(
            jnp.where(row == column, lower, 0.0), axis=0, keepdims=True
        )
    mom = mom_ref[...]
    out_ref[MOMENT_ROW : MOMENT_ROW + N_BASIS, 0:P_COV] = mom[0:8, 0:P_COV] + mom[8:16, 0:P_COV] + mom[0:8, P_COV:]


def local_sums(count, covariates, intervals, offsets, responses):
    slots = covariates.shape[1]
    in_place = pl.BlockSpec(memory_space=pltpu.HBM)
    design = pltpu.VMEM((WIDTH, CHUNK), BF16)
    return pl.pallas_call(
        gram_kernel,
        in_specs=[pl.BlockSpec(memory_space=pltpu.SMEM), in_place, in_place, in_place, in_place],
        out_shape=jax.ShapeDtypeStruct((SLAB_ROWS, 128), F32),
        scratch_shapes=[
            pltpu.VMEM((P_COV, slots), F32),
            pltpu.VMEM((1, slots), jnp.int32),
            pltpu.VMEM((1, slots), F32),
            pltpu.VMEM((1, slots), F32),
            design,
            design,
            design,
            design,
            pltpu.VMEM((WIDTH, WIDTH), F32),
            pltpu.VMEM((WIDTH, WIDTH), F32),
            pltpu.VMEM((16, 128), F32),
            pltpu.SemaphoreType.DMA((3,)),
            pltpu.SemaphoreType.DMA((2,)),
        ],
        compiler_params=pltpu.CompilerParams(vmem_limit_bytes=62 * 1024 * 1024),
        name="local_sums",
    )(count, covariates, intervals[None, :], offsets[None, :], responses[None, :])


def sum_repeat_kernel(parts, copies, in_ref, out_ref):
    rows = in_ref.shape[0] // parts
    total = in_ref[0:rows, :]
    for i in range(1, parts):
        total = total + in_ref[i * rows : (i + 1) * rows, :]
    for i in range(copies):
        out_ref[i * rows : (i + 1) * rows, :] = total


def sum_repeat(received, parts, copies):
    rows = received.shape[0] // parts
    return pl.pallas_call(
        lambda a, b: sum_repeat_kernel(parts, copies, a, b),
        out_shape=jax.ShapeDtypeStruct((copies * rows, 128), F32),
        compiler_params=pltpu.CompilerParams(vmem_limit_bytes=4 * 1024 * 1024),
        name="sum_repeat",
    )(received)


def lane_spread(tile, lane):
    return jnp.take_along_axis(tile, jnp.full(tile.shape, lane, jnp.int32), axis=1)


def row_spread(tile, row):
    return jnp.broadcast_to(tile[row : row + 1, :], tile.shape)


def factor_tile(work, side):
    blocks = len(work)
    lanes = lax.broadcasted_iota(jnp.int32, (8, 128), 1)
    subs = lax.broadcasted_iota(jnp.int32, (8, 128), 0)
    factor_rows, inverse_rows = [], []
    for k in range(blocks):
        columns = [lane_spread(work[k], 8 * k + t) for t in range(8)]
        entry = {(s, t): row_spread(columns[t], s) for t in range(8) for s in range(t, 8)}
        rows = [row_spread(work[k], t) for t in range(8)]
        siderows = [row_spread(side[k], t) for t in range(8)]
        reciprocals, scale = [], {}
        for t in range(8):
            reciprocals.append(1.0 / entry[t, t])
            for s in range(t + 1, 8):
                scale[s, t] = entry[s, t] * reciprocals[t]
            for s in range(t + 1, 8):
                for u in range(t + 1, s + 1):
                    entry[s, u] = entry[s, u] - scale[s, t] * entry[u, t]
                rows[s] = rows[s] - scale[s, t] * rows[t]
                siderows[s] = siderows[s] - scale[s, t] * siderows[t]
        for b in range(k + 1, blocks):
            c = [lane_spread(work[b], 8 * k + t) for t in range(8)]
            for t in range(8):
                for s in range(t + 1, 8):
                    c[s] = c[s] - scale[s, t] * c[t]
                weight = c[t] * reciprocals[t]
                work[b] = work[b] - weight * rows[t]
                side[b] = side[b] - weight * siderows[t]
        out, sideout = jnp.zeros((8, 128), F32), jnp.zeros((8, 128), F32)
        for t in range(8):
            root = lax.rsqrt(entry[t, t])
            out = jnp.where(subs == t, rows[t] * root, out)
            sideout = jnp.where(subs == t, siderows[t] * root, sideout)
        factor_rows.append(jnp.where(lanes >= subs + 8 * k, out, 0.0))
        inverse_rows.append(jnp.where(lanes <= subs + 8 * k, sideout, 0.0))
    return factor_rows, inverse_rows


def factor_kernel(sums_ref, smooth_ref, factor_ref, proj_ref, half_ref, gram_ref, inv_ref):
    row, column, left = slab_masks()
    second = np.zeros((N_BASIS - 2, N_BASIS))
    for i in range(N_BASIS - 2):
        second[i, i : i + 3] = (1.0, -2.0, 1.0)
    penalty = second.T @ second
    smooth = jnp.where(row == column, jnp.concatenate([smooth_ref[...], smooth_ref[...]], axis=1), 0.0)
    slabs, place = {}, {}

    def keep(entry, value):
        w, j_left, j_right = entry
        scale = jnp.where(left, float(penalty[j_left, 2 * w]), float(penalty[j_right, 2 * w + 1]))
        slabs[entry] = value * (1.0 / TOTAL_LIVE) + smooth * scale
        place[j_left, 2 * w] = entry
        if j_right >= 2 * w + 1:
            place[j_right, 2 * w + 1] = entry

    for i in range(HALF):
        packed = sums_ref[i * P_COV : (i + 1) * P_COV, :]
        turned = jnp.concatenate([packed[:, :P_COV].T, packed[:, P_COV:].T], axis=1)
        keep(ROW_SLABS[i], jnp.where(row <= column, packed, turned))
        diagonal = jnp.broadcast_to(sums_ref[DIAG_ROW + i : DIAG_ROW + i + 1, :], (P_COV, 128))
        keep(ROW_SLABS[HALF + i], jnp.where(row == column, diagonal, jnp.where(row > column, packed, turned)))
    swapped = {}

    def in_half(j, k, half):
        pair = (max(j, k), min(j, k))
        if pair not in place:
            return None
        entry = place[pair]
        if pair[1] % 2 == half:
            return slabs[entry]
        if entry not in swapped:
            swapped[entry] = pltpu.roll(slabs[entry], P_COV, 1)
        return swapped[entry]

    nothing = jnp.zeros((P_COV, 128), F32)
    for j in range(N_BASIS):
        for w in range(4):
            first, second = in_half(j, 2 * w, 0), in_half(j, 2 * w + 1, 1)
            first, second = (nothing if first is None else first), (nothing if second is None else second)
            half_ref[w, pl.ds(j, P_COV, N_BASIS), :] = first if first is second else jnp.where(left, first, second)
    for w in range(4):
        for i in range(4):
            turned = half_ref[w, 128 * i : 128 * i + 128, :].T
            for k in (2 * w, 2 * w + 1):
                gram_ref[i, pl.ds(k, P_COV, N_BASIS), :] = turned[(k - 2 * w) * P_COV : (k - 2 * w + 1) * P_COV, :]
    moment = sums_ref[MOMENT_ROW : MOMENT_ROW + N_BASIS, 0:P_COV].T * (1.0 / math.sqrt(TOTAL_LIVE))
    for j in range(N_BASIS):
        gram_ref[4, pl.ds(j, P_COV, N_BASIS), :] = jnp.broadcast_to(moment[:, j : j + 1], (P_COV, 128))

    factor_ref[...] = jnp.zeros_like(factor_ref)
    lanes = lax.broadcasted_iota(jnp.int32, (8, 128), 1)
    subs = lax.broadcasted_iota(jnp.int32, (8, 128), 0)

    def panel(p, _):
        start = pl.multiple_of(p * 128, 128)
        work = [gram_ref[p, pl.ds(pl.multiple_of(start + 8 * b, 8), 8), :] for b in range(16)]
        side = [jnp.where(lanes == subs + 8 * b, 1.0, 0.0).astype(F32) for b in range(16)]
        factor_rows, inverse_rows = factor_tile(work, side)
        for b in range(16):
            inv_ref[8 * b : 8 * b + 8, :] = inverse_rows[b]
            factor_ref[pl.ds(pl.multiple_of(start + 8 * b, 8), 8), pl.ds(start, 128)] = factor_rows[b]

        for q in range(4):

            @pl.when(p == q)
            def _():
                mine = slice(128 * q, 128 * q + 128)
                inverse = inv_ref[...]
                solved = {}
                for w in range(q + 1, 5):
                    solved[w] = jnp.dot(inverse, gram_ref[w, mine, :], precision=HIGHEST, preferred_element_type=F32)
                    gram_ref[w, mine, :] = solved[w]
                    if w < 4:
                        factor_ref[mine, 128 * w : 128 * w + 128] = solved[w]
                for i in range(q + 1, 4):
                    for w in range(i, 5):
                        gram_ref[w, 128 * i : 128 * i + 128, :] -= lax.dot_general(
                            solved[i], solved[w], TN, precision=HIGHEST, preferred_element_type=F32
                        )

        return 0

    lax.fori_loop(0, 4, panel, 0)
    diagonal_mask = lax.broadcasted_iota(jnp.int32, (128, 128), 0) == lax.broadcasted_iota(jnp.int32, (128, 128), 1)
    for p in range(4):
        tile = gram_ref[4, 128 * p : 128 * p + 128, :]
        proj_ref[:, 128 * p : 128 * p + 128] = jnp.sum(jnp.where(diagonal_mask, tile, 0.0), axis=0, keepdims=True)


def factorize(sums, smoothing):
    return pl.pallas_call(
        factor_kernel,
        out_shape=(
            jax.ShapeDtypeStruct((WIDTH, WIDTH), F32),
            jax.ShapeDtypeStruct((1, WIDTH), F32),
        ),
        scratch_shapes=[
            pltpu.VMEM((4, WIDTH, 128), F32),
            pltpu.VMEM((5, WIDTH, 128), F32),
            pltpu.VMEM((128, 128), F32),
        ],
        compiler_params=pltpu.CompilerParams(vmem_limit_bytes=40 * 1024 * 1024),
        name="factorize",
    )(sums, smoothing[None, :])


NEAR = ("zn", "yn", "core", "x")
FAR = ("zf", "yf")


def exchange(rows, axes, parts):
    return lax.all_to_all(rows.reshape(parts, -1, 128), axes, 0, 0, tiled=True).reshape(-1, 128)


def per_device(covariates, intervals, offsets, responses, counts, smoothing):
    sums = local_sums(counts, covariates, intervals, offsets, responses)
    shares = sum_repeat(exchange(sums, NEAR, SHARES), SHARES, 16)
    shares = sum_repeat(exchange(shares, FAR, 16), 16, SHARES)
    factor, projected = factorize(exchange(shares, NEAR, SHARES), smoothing)
    return factor, projected[0]


def solution(mesh):
    fine = Mesh(mesh.devices.reshape(4, 2, 4, 2, 2, 4), ("zf", "zn", "yf", "yn", "core", "x"))
    spread = fine.axis_names
    return jax.shard_map(
        per_device,
        mesh=fine,
        in_specs=(P(None, spread), P(spread), P(spread), P(spread), P(spread), P()),
        out_specs=(P(), P()),
        check_vma=False,
    )
```

```python
import math

import jax
import jax.numpy as jnp
import numpy as np
from jax import lax
from jax.experimental import pallas as pl
from jax.experimental.pallas import tpu as pltpu
from jax.sharding import Mesh, PartitionSpec as P

P_COV = 64
N_BASIS = 8
WIDTH = P_COV * N_BASIS
CHUNK = 1024
TOTAL_LIVE = 2097152
F32 = jnp.float32
BF16 = jnp.bfloat16
HIGHEST = lax.Precision.HIGHEST

ROW_SLABS = [(0, 0, 4), (0, 1, 1), (0, 2, 2), (0, 3, 3), (1, 2, 6), (1, 3, 3), (1, 4, 4), (1, 5, 5)]
ROW_SLABS += [(2, 4, 4), (2, 5, 5), (2, 6, 6), (2, 7, 7), (3, 6, 6), (3, 7, 7)]
HALF = len(ROW_SLABS) // 2
SHARES = 32
SHARE_ROWS = 16
SLAB_ROWS = SHARES * SHARE_ROWS
DIAG_ROW = HALF * P_COV
MOMENT_ROW = DIAG_ROW + 8
NT = (((1,), (1,)), ((), ()))
TN = (((0,), (0,)), ((), ()))


def slab_masks():
    row = lax.broadcasted_iota(jnp.int32, (P_COV, 128), 0)
    column = lax.broadcasted_iota(jnp.int32, (P_COV, 128), 1)
    return row, column % P_COV, column < P_COV


def gram_kernel(
    count_ref, cov_hbm, int_hbm, off_hbm, resp_hbm, out_ref,
    cov_ref, int_ref, off_ref, resp_ref, hi_even, hi_odd, lo_even, lo_odd, hh_ref, lh_ref, mom_ref, row_sem, cov_sem,
):
    count = count_ref[0]
    chunks = cov_hbm.shape[1] // CHUNK

    def columns(c):
        return pl.ds(pl.multiple_of(c * CHUNK, CHUNK), CHUNK)

    row_copies = [
        pltpu.make_async_copy(source, target, row_sem.at[i])
        for i, (source, target) in enumerate([(int_hbm, int_ref), (off_hbm, off_ref), (resp_hbm, resp_ref)])
    ]
    cov_copies = [
        pltpu.make_async_copy(cov_hbm.at[:, part], cov_ref.at[:, part], cov_sem.at[i])
        for i, part in enumerate([slice(0, CHUNK), slice(CHUNK, chunks * CHUNK)])
    ]
    for copy in [*row_copies, *cov_copies]:
        copy.start()
    hh_ref[...] = jnp.zeros_like(hh_ref)
    lh_ref[...] = jnp.zeros_like(lh_ref)
    mom_ref[...] = jnp.zeros_like(mom_ref)
    for copy in row_copies:
        copy.wait()

    def build(c, hi_ref, lo_ref):
        part = columns(jnp.minimum(c, chunks - 1))
        cov = cov_ref[:, part]
        interval = int_ref[:, part]
        within = off_ref[:, part]
        slot = lax.broadcasted_iota(jnp.int32, (1, CHUNK), 1) + c * CHUNK
        live = jnp.where(slot < count, 1.0, 0.0).astype(F32)
        square = within * within
        cube = square * within
        rest = 1.0 - within
        first = rest * rest * rest * (1.0 / 6.0) * live
        second = (3.0 * cube - 6.0 * square + 4.0) * (1.0 / 6.0) * live
        third = (-3.0 * cube + 3.0 * square + 3.0 * within + 1.0) * (1.0 / 6.0) * live
        fourth = cube * (1.0 / 6.0) * live
        weights = []
        for j in range(N_BASIS):
            value = jnp.where(interval == j, first, 0.0)
            value = jnp.where(interval + 1 == j, second, value)
            value = jnp.where(interval + 2 == j, third, value)
            value = jnp.where(interval + 3 == j, fourth, value)
            weights.append(value)
            design = cov * value
            high = design.astype(BF16)
            hi_ref[j * P_COV : (j + 1) * P_COV, :] = high
            lo_ref[j * P_COV : (j + 1) * P_COV, :] = (design - high.astype(F32)).astype(BF16)
        cov_high = cov.astype(BF16)
        cov_low = (cov - cov_high.astype(F32)).astype(BF16)
        weighted = jnp.concatenate(weights, axis=0) * resp_ref[:, part]
        weighted_high = weighted.astype(BF16)
        weighted_low = (weighted - weighted_high.astype(F32)).astype(BF16)
        mom_ref[...] += lax.dot_general(
            jnp.concatenate([weighted_high, weighted_low], axis=0),
            jnp.concatenate([cov_high, cov_low], axis=0),
            NT,
            preferred_element_type=F32,
        )

    def multiply(hi_ref, lo_ref):
        def product(left_ref, rows, columns):
            return lax.dot_general(left_ref[rows, :], hi_ref[columns, :], NT, preferred_element_type=F32)

        low, high_half = slice(0, 256), slice(256, 512)
        hh_ref[0:448, low] += product(hi_ref, slice(0, 448), low)
        lh_ref[0:448, low] += product(lo_ref, slice(0, 448), low)
        hh_ref[high_half, high_half] += product(hi_ref, high_half, high_half)
        lh_ref[64:512, high_half] += product(lo_ref, slice(64, 512), high_half)

    cov_copies[0].wait()
    build(0, hi_even, lo_even)
    cov_copies[1].wait()

    def pair(i, _):
        build(2 * i + 1, hi_odd, lo_odd)
        multiply(hi_even, lo_even)
        build(2 * i + 2, hi_even, lo_even)
        multiply(hi_odd, lo_odd)
        return 0

    lax.fori_loop(0, pl.cdiv(count, 2 * CHUNK), pair, 0)

    row, column, left = slab_masks()
    tiles = {}

    def row_slab(entry):
        w, j_left, j_right = entry
        pieces = []
        for j in (j_left, j_right):
            t = j // 2
            if (t, w) not in tiles:
                at, across = slice(128 * t, 128 * t + 128), slice(128 * w, 128 * w + 128)
                tiles[t, w] = hh_ref[at, across] + lh_ref[at, across] + lh_ref[across, at].T
            pieces.append(tiles[t, w][(j % 2) * P_COV : (j % 2 + 1) * P_COV, :])
        return pieces[0] if j_left == j_right else jnp.where(left, pieces[0], pieces[1])

    out_ref[DIAG_ROW:, :] = jnp.zeros((SLAB_ROWS - DIAG_ROW, 128), F32)
    for i in range(HALF):
        upper, lower = row_slab(ROW_SLABS[i]), row_slab(ROW_SLABS[HALF + i])
        out_ref[i * P_COV : (i + 1) * P_COV, :] = jnp.where(row <= column, upper, lower)
        out_ref[DIAG_ROW + i : DIAG_ROW + i + 1, :] = jnp.sum(
            jnp.where(row == column, lower, 0.0), axis=0, keepdims=True
        )
    mom = mom_ref[...]
    out_ref[MOMENT_ROW : MOMENT_ROW + N_BASIS, 0:P_COV] = mom[0:8, 0:P_COV] + mom[8:16, 0:P_COV] + mom[0:8, P_COV:]


def local_sums(count, covariates, intervals, offsets, responses):
    slots = covariates.shape[1]
    in_place = pl.BlockSpec(memory_space=pltpu.HBM)
    design = pltpu.VMEM((WIDTH, CHUNK), BF16)
    return pl.pallas_call(
        gram_kernel,
        in_specs=[pl.BlockSpec(memory_space=pltpu.SMEM), in_place, in_place, in_place, in_place],
        out_shape=jax.ShapeDtypeStruct((SLAB_ROWS, 128), F32),
        scratch_shapes=[
            pltpu.VMEM((P_COV, slots), F32),
            pltpu.VMEM((1, slots), jnp.int32),
            pltpu.VMEM((1, slots), F32),
            pltpu.VMEM((1, slots), F32),
            design,
            design,
            design,
            design,
            pltpu.VMEM((WIDTH, WIDTH), F32),
            pltpu.VMEM((WIDTH, WIDTH), F32),
            pltpu.VMEM((16, 128), F32),
            pltpu.SemaphoreType.DMA((3,)),
            pltpu.SemaphoreType.DMA((2,)),
        ],
        compiler_params=pltpu.CompilerParams(vmem_limit_bytes=62 * 1024 * 1024),
        name="local_sums",
    )(count, covariates, intervals[None, :], offsets[None, :], responses[None, :])


def sum_repeat_kernel(parts, copies, in_ref, out_ref):
    rows = in_ref.shape[0] // parts
    total = in_ref[0:rows, :]
    for i in range(1, parts):
        total = total + in_ref[i * rows : (i + 1) * rows, :]
    for i in range(copies):
        out_ref[i * rows : (i + 1) * rows, :] = total


def sum_repeat(received, parts, copies):
    rows = received.shape[0] // parts
    return pl.pallas_call(
        lambda a, b: sum_repeat_kernel(parts, copies, a, b),
        out_shape=jax.ShapeDtypeStruct((copies * rows, 128), F32),
        compiler_params=pltpu.CompilerParams(vmem_limit_bytes=4 * 1024 * 1024),
        name="sum_repeat",
    )(received)


def lane_spread(tile, lane):
    return jnp.take_along_axis(tile, jnp.full(tile.shape, lane, jnp.int32), axis=1)


def row_spread(tile, row):
    return jnp.broadcast_to(tile[row : row + 1, :], tile.shape)


def three_terms(value):
    high = value.astype(BF16)
    rest = value - high.astype(F32)
    middle = rest.astype(BF16)
    return high, middle, (rest - middle.astype(F32)).astype(BF16)


def float_product_tn(left, right):
    a, b = three_terms(left), three_terms(right)
    order = [(0, 0), (0, 1), (1, 0), (1, 1), (0, 2), (2, 0)]
    return lax.dot_general(
        jnp.concatenate([a[i] for i, _ in order], axis=0),
        jnp.concatenate([b[i] for _, i in order], axis=0),
        TN,
        preferred_element_type=F32,
    )


def factor_tile(work, side):
    blocks = len(work)
    lanes = lax.broadcasted_iota(jnp.int32, (8, 128), 1)
    subs = lax.broadcasted_iota(jnp.int32, (8, 128), 0)
    factor_rows, inverse_rows = [], []
    for k in range(blocks):
        if k == 0:
            columns = [lane_spread(work[0], t) for t in range(8)]
        if k + 1 < blocks:
            ahead = [lane_spread(work[k + 1], 8 * k + 8 + t) for t in range(8)]
        entry = {(s, t): row_spread(columns[t], s) for t in range(8) for s in range(t, 8)}
        rows = [row_spread(work[k], t) for t in range(8)]
        siderows = [row_spread(side[k], t) for t in range(8)]
        pivot = entry[0, 0]
        pivots, reciprocals, scale = [], [], {}
        for t in range(8):
            reciprocal = 1.0 / pivot
            pivots.append(pivot)
            reciprocals.append(reciprocal)
            if t + 1 < 8:
                pivot = entry[t + 1, t + 1] - (entry[t + 1, t] * entry[t + 1, t]) * reciprocal
            for s in range(t + 1, 8):
                scale[s, t] = entry[s, t] * reciprocal
            for s in range(t + 1, 8):
                for u in range(t + 1, s + 1):
                    if (s, u) != (t + 1, t + 1):
                        entry[s, u] = entry[s, u] - scale[s, t] * entry[u, t]
                rows[s] = rows[s] - scale[s, t] * rows[t]
                siderows[s] = siderows[s] - scale[s, t] * siderows[t]
        near = k + 3 if k % 2 else k + 4
        for b in range(k + 1, min(near, blocks)):
            c = [lane_spread(work[b], 8 * k + t) for t in range(8)]
            for t in range(8):
                for s in range(t + 1, 8):
                    c[s] = c[s] - scale[s, t] * c[t]
                weight = c[t] * reciprocals[t]
                work[b] = work[b] - weight * rows[t]
                side[b] = side[b] - weight * siderows[t]
                if b == k + 1:
                    ahead = [ahead[u] - weight * row_spread(c[t], u) for u in range(8)]
        if k + 1 < blocks:
            columns = ahead
        out, sideout = jnp.zeros((8, 128), F32), jnp.zeros((8, 128), F32)
        for t in range(8):
            root = lax.rsqrt(pivots[t])
            out = jnp.where(subs == t, rows[t] * root, out)
            sideout = jnp.where(subs == t, siderows[t] * root, sideout)
        factor_rows.append(jnp.where(lanes >= subs + 8 * k, out, 0.0))
        inverse_rows.append(jnp.where(lanes <= subs + 8 * k, sideout, 0.0))
        if k % 2 and near < blocks:
            upper = jnp.concatenate(factor_rows[k - 1 :], axis=0)
            both = jnp.concatenate([upper, jnp.concatenate(inverse_rows[k - 1 :], axis=0)], axis=1)
            change = float_product_tn(upper, both)
            for b in range(near, blocks):
                work[b] = work[b] - change[8 * b : 8 * b + 8, :128]
                side[b] = side[b] - change[8 * b : 8 * b + 8, 128:]
    return factor_rows, inverse_rows


def factor_kernel(sums_ref, smooth_ref, factor_ref, proj_ref, half_ref, gram_ref, inv_ref):
    row, column, left = slab_masks()
    second = np.zeros((N_BASIS - 2, N_BASIS))
    for i in range(N_BASIS - 2):
        second[i, i : i + 3] = (1.0, -2.0, 1.0)
    penalty = second.T @ second
    smooth = jnp.where(row == column, jnp.concatenate([smooth_ref[...], smooth_ref[...]], axis=1), 0.0)
    slabs, place = {}, {}

    def keep(entry, value):
        w, j_left, j_right = entry
        scale = jnp.where(left, float(penalty[j_left, 2 * w]), float(penalty[j_right, 2 * w + 1]))
        slabs[entry] = value * (1.0 / TOTAL_LIVE) + smooth * scale
        place[j_left, 2 * w] = entry
        if j_right >= 2 * w + 1:
            place[j_right, 2 * w + 1] = entry

    for i in range(HALF):
        packed = sums_ref[i * P_COV : (i + 1) * P_COV, :]
        turned = jnp.concatenate([packed[:, :P_COV].T, packed[:, P_COV:].T], axis=1)
        keep(ROW_SLABS[i], jnp.where(row <= column, packed, turned))
        diagonal = jnp.broadcast_to(sums_ref[DIAG_ROW + i : DIAG_ROW + i + 1, :], (P_COV, 128))
        keep(ROW_SLABS[HALF + i], jnp.where(row == column, diagonal, jnp.where(row > column, packed, turned)))
    swapped = {}

    def in_half(j, k, half):
        pair = (max(j, k), min(j, k))
        if pair not in place:
            return None
        entry = place[pair]
        if pair[1] % 2 == half:
            return slabs[entry]
        if entry not in swapped:
            swapped[entry] = pltpu.roll(slabs[entry], P_COV, 1)
        return swapped[entry]

    nothing = jnp.zeros((P_COV, 128), F32)
    for j in range(N_BASIS):
        for w in range(4):
            first, second = in_half(j, 2 * w, 0), in_half(j, 2 * w + 1, 1)
            first, second = (nothing if first is None else first), (nothing if second is None else second)
            half_ref[w, pl.ds(j, P_COV, N_BASIS), :] = first if first is second else jnp.where(left, first, second)
    for w in range(4):
        for i in range(4):
            turned = half_ref[w, 128 * i : 128 * i + 128, :].T
            above = 16 * (i + 1)
            for k in (2 * w, 2 * w + 1):
                gram_ref[i, pl.ds(k, above, N_BASIS), :] = turned[(k - 2 * w) * P_COV : (k - 2 * w) * P_COV + above, :]
    moment = sums_ref[MOMENT_ROW : MOMENT_ROW + N_BASIS, 0:P_COV].T * (1.0 / math.sqrt(TOTAL_LIVE))
    for j in range(N_BASIS):
        gram_ref[4, pl.ds(j, P_COV, N_BASIS), :] = jnp.broadcast_to(moment[:, j : j + 1], (P_COV, 128))

    factor_ref[...] = jnp.zeros_like(factor_ref)
    lanes = lax.broadcasted_iota(jnp.int32, (8, 128), 1)
    subs = lax.broadcasted_iota(jnp.int32, (8, 128), 0)

    def panel(p, _):
        start = pl.multiple_of(p * 128, 128)
        work = [gram_ref[p, pl.ds(pl.multiple_of(start + 8 * b, 8), 8), :] for b in range(16)]
        side = [jnp.where(lanes == subs + 8 * b, 1.0, 0.0).astype(F32) for b in range(16)]
        factor_rows, inverse_rows = factor_tile(work, side)
        for b in range(16):
            inv_ref[8 * b : 8 * b + 8, :] = inverse_rows[b]
            factor_ref[pl.ds(pl.multiple_of(start + 8 * b, 8), 8), pl.ds(start, 128)] = factor_rows[b]

        for q in range(4):

            @pl.when(p == q)
            def _():
                mine = slice(128 * q, 128 * q + 128)
                inverse = inv_ref[...]
                solved = {}
                for w in range(q + 1, 5):
                    solved[w] = jnp.dot(inverse, gram_ref[w, mine, :], precision=HIGHEST, preferred_element_type=F32)
                    gram_ref[w, mine, :] = solved[w]
                    if w < 4:
                        factor_ref[mine, 128 * w : 128 * w + 128] = solved[w]
                for i in range(q + 1, 4):
                    for w in range(i, 5):
                        gram_ref[w, 128 * i : 128 * i + 128, :] -= lax.dot_general(
                            solved[i], solved[w], TN, precision=HIGHEST, preferred_element_type=F32
                        )

        return 0

    lax.fori_loop(0, 4, panel, 0)
    diagonal_mask = lax.broadcasted_iota(jnp.int32, (128, 128), 0) == lax.broadcasted_iota(jnp.int32, (128, 128), 1)
    for p in range(4):
        tile = gram_ref[4, 128 * p : 128 * p + 128, :]
        proj_ref[:, 128 * p : 128 * p + 128] = jnp.sum(jnp.where(diagonal_mask, tile, 0.0), axis=0, keepdims=True)


def factorize(sums, smoothing):
    return pl.pallas_call(
        factor_kernel,
        out_shape=(
            jax.ShapeDtypeStruct((WIDTH, WIDTH), F32),
            jax.ShapeDtypeStruct((1, WIDTH), F32),
        ),
        scratch_shapes=[
            pltpu.VMEM((4, WIDTH, 128), F32),
            pltpu.VMEM((5, WIDTH, 128), F32),
            pltpu.VMEM((128, 128), F32),
        ],
        compiler_params=pltpu.CompilerParams(vmem_limit_bytes=40 * 1024 * 1024),
        name="factorize",
    )(sums, smoothing[None, :])


NEAR = ("zn", "yn", "core", "x")
FAR = ("zf", "yf")


def exchange(rows, axes, parts):
    return lax.all_to_all(rows.reshape(parts, -1, 128), axes, 0, 0, tiled=True).reshape(-1, 128)


def per_device(covariates, intervals, offsets, responses, counts, smoothing):
    sums = local_sums(counts, covariates, intervals, offsets, responses)
    shares = sum_repeat(exchange(sums, NEAR, SHARES), SHARES, 16)
    shares = sum_repeat(exchange(shares, FAR, 16), 16, SHARES)
    factor, projected = factorize(exchange(shares, NEAR, SHARES), smoothing)
    return factor, projected[0]


def solution(mesh):
    fine = Mesh(mesh.devices.reshape(4, 2, 4, 2, 2, 4), ("zf", "zn", "yf", "yn", "core", "x"))
    spread = fine.axis_names
    return jax.shard_map(
        per_device,
        mesh=fine,
        in_specs=(P(None, spread), P(spread), P(spread), P(spread), P(spread), P()),
        out_specs=(P(), P()),
        check_vma=False,
    )
```

```python
import math

import jax
import jax.numpy as jnp
import numpy as np
from jax import lax
from jax.experimental import pallas as pl
from jax.experimental.pallas import tpu as pltpu
from jax.sharding import Mesh, PartitionSpec as P

P_COV = 64
N_BASIS = 8
WIDTH = P_COV * N_BASIS
CHUNK = 2048
UNROLL = 2
TOTAL_LIVE = 2097152
F32 = jnp.float32
BF16 = jnp.bfloat16
HIGHEST = lax.Precision.HIGHEST

ROW_SLABS = [(0, 0, 4), (0, 1, 1), (0, 2, 2), (0, 3, 3), (1, 2, 6), (1, 3, 3), (1, 4, 4), (1, 5, 5)]
ROW_SLABS += [(2, 4, 4), (2, 5, 5), (2, 6, 6), (2, 7, 7), (3, 6, 6), (3, 7, 7)]
HALF = len(ROW_SLABS) // 2
SHARES = 32
SHARE_ROWS = 16
SLAB_ROWS = SHARES * SHARE_ROWS
DIAG_ROW = HALF * P_COV
MOMENT_ROW = DIAG_ROW + 8
NT = (((1,), (1,)), ((), ()))
TN = (((0,), (0,)), ((), ()))


HI_SUMS = [(0, 7), (0, 6), (1, 7)]
LO_SUMS = [(0, 7), (0, 5), (1, 6), (2, 7)]
MID_ROWS = [8, 1, 6, 2, 3, 4, 5]
MID_PLACE = {0: 0, 7: 0, 1: 1, 6: 2, 2: 3, 3: 4, 4: 5, 5: 6}
END_HI_ROWS = [9, 10]
END_LO_ROWS = [9, 10, 11, 3, 4]


def basis_rows(j):
    return slice(j * P_COV, (j + 1) * P_COV)


def slab_masks():
    row = lax.broadcasted_iota(jnp.int32, (P_COV, 128), 0)
    column = lax.broadcasted_iota(jnp.int32, (P_COV, 128), 1)
    return row, column % P_COV, column < P_COV


def gram_kernel(
    count_ref, cov_hbm, int_hbm, off_hbm, resp_hbm, out_ref,
    cov_ref, int_ref, off_ref, resp_ref, hi_even, hi_odd, lo_even, lo_odd, mid_ref, end_ref, mom_ref, row_sem, cov_sem,
):
    count = count_ref[0]
    chunks = cov_hbm.shape[1] // CHUNK

    def columns(c):
        return pl.ds(pl.multiple_of(c * CHUNK, CHUNK), CHUNK)

    row_copies = [
        pltpu.make_async_copy(source, target, row_sem.at[i])
        for i, (source, target) in enumerate([(int_hbm, int_ref), (off_hbm, off_ref), (resp_hbm, resp_ref)])
    ]
    groups = chunks // UNROLL

    def cov_copy(i):
        part = pl.ds(pl.multiple_of(i * UNROLL * CHUNK, UNROLL * CHUNK), UNROLL * CHUNK)
        return pltpu.make_async_copy(cov_hbm.at[:, part], cov_ref.at[:, part], cov_sem.at[i])

    for copy in row_copies:
        copy.start()
    for i in range(groups):
        cov_copy(i).start()
    mid_ref[...] = jnp.zeros_like(mid_ref)
    end_ref[...] = jnp.zeros_like(end_ref)
    mom_ref[...] = jnp.zeros_like(mom_ref)
    for copy in row_copies:
        copy.wait()

    def build(c, hi_ref, lo_ref):
        part = columns(c)
        cov = cov_ref[:, part]
        interval = int_ref[:, part]
        within = off_ref[:, part]
        slot = lax.broadcasted_iota(jnp.int32, (1, CHUNK), 1) + c * CHUNK
        live = jnp.where(slot < count, 1.0, 0.0).astype(F32)
        square = within * within
        cube = square * within
        rest = 1.0 - within
        first = rest * rest * rest * (1.0 / 6.0) * live
        second = (3.0 * cube - 6.0 * square + 4.0) * (1.0 / 6.0) * live
        third = (-3.0 * cube + 3.0 * square + 3.0 * within + 1.0) * (1.0 / 6.0) * live
        fourth = cube * (1.0 / 6.0) * live
        weights, highs, lows = [], [], []
        for j in range(N_BASIS):
            value = jnp.where(interval == j, first, 0.0)
            value = jnp.where(interval + 1 == j, second, value)
            value = jnp.where(interval + 2 == j, third, value)
            value = jnp.where(interval + 3 == j, fourth, value)
            weights.append(value)
            design = cov * value
            highs.append(design.astype(BF16))
            lows.append((design - highs[j].astype(F32)).astype(BF16))
            hi_ref[basis_rows(j), :] = highs[j]
            lo_ref[basis_rows(j), :] = lows[j]
        for i, (j, k) in enumerate(HI_SUMS):
            hi_ref[basis_rows(N_BASIS + i), :] = highs[j] + highs[k]
        for i, (j, k) in enumerate(LO_SUMS):
            lo_ref[basis_rows(N_BASIS + i), :] = lows[j] + lows[k]
        cov_high = cov.astype(BF16)
        cov_low = (cov - cov_high.astype(F32)).astype(BF16)
        weighted = jnp.concatenate(weights, axis=0) * resp_ref[:, part]
        weighted_high = weighted.astype(BF16)
        weighted_low = (weighted - weighted_high.astype(F32)).astype(BF16)
        mom_ref[...] += lax.dot_general(
            jnp.concatenate([weighted_high, weighted_low], axis=0),
            jnp.concatenate([cov_high, cov_low], axis=0),
            NT,
            preferred_element_type=F32,
        )

    def multiply(hi_ref, lo_ref):
        def rows_of(ref, places):
            return [ref[basis_rows(place), :] for place in places]

        middle = jnp.concatenate(rows_of(hi_ref, MID_ROWS) + rows_of(lo_ref, MID_ROWS), axis=0)
        mid_ref[...] += lax.dot_general(middle, hi_ref[128:384, :], NT, preferred_element_type=F32)
        ends = jnp.concatenate(rows_of(hi_ref, END_HI_ROWS) + rows_of(lo_ref, END_LO_ROWS), axis=0)
        across = jnp.concatenate([hi_ref[0:128, :], hi_ref[384:512, :]], axis=0)
        end_ref[...] += lax.dot_general(ends, across, NT, preferred_element_type=F32)

    def group(i, _):
        cov_copy(i).wait()
        for c in range(UNROLL):
            hi_ref, lo_ref = (hi_odd, lo_odd) if c % 2 else (hi_even, lo_even)
            build(UNROLL * i + c, hi_ref, lo_ref)
            multiply(hi_ref, lo_ref)
        return 0

    def unused(i, _):
        cov_copy(i).wait()
        return 0

    used = pl.cdiv(count, UNROLL * CHUNK)
    lax.fori_loop(0, used, group, 0)
    lax.fori_loop(used, groups, unused, 0)

    row, column, left = slab_masks()
    tiles = {}

    def high_rows(j, w):
        if w in (1, 2):
            return mid_ref[basis_rows(MID_PLACE[j]), 128 * w - 128 : 128 * w]
        return end_ref[basis_rows(j % 6), 0:128] if w == 0 else end_ref[basis_rows(j - 6), 128:256]

    def low_rows(j, w):
        if w in (1, 2):
            return mid_ref[basis_rows(len(MID_ROWS) + MID_PLACE[j]), 128 * w - 128 : 128 * w]
        place = len(END_HI_ROWS) + (j if j < 5 else j - 5)
        return end_ref[basis_rows(place), 0:128] if w == 0 else end_ref[basis_rows(place), 128:256]

    def tile(t, w):
        turn_high = w == 0 and t in (1, 2)
        straight = [low_rows(j, w) if turn_high else low_rows(j, w) + high_rows(j, w) for j in (2 * t, 2 * t + 1)]
        turned = [low_rows(k, t) + high_rows(k, t) if turn_high else low_rows(k, t) for k in (2 * w, 2 * w + 1)]
        return jnp.concatenate(straight, axis=0) + jnp.concatenate(turned, axis=0).T

    def row_slab(entry):
        w, j_left, j_right = entry
        pieces = []
        for j in (j_left, j_right):
            t = j // 2
            if (t, w) not in tiles:
                tiles[t, w] = tile(t, w)
            pieces.append(tiles[t, w][(j % 2) * P_COV : (j % 2 + 1) * P_COV, :])
        return pieces[0] if j_left == j_right else jnp.where(left, pieces[0], pieces[1])

    out_ref[DIAG_ROW:, :] = jnp.zeros((SLAB_ROWS - DIAG_ROW, 128), F32)
    for i in range(HALF):
        upper, lower = row_slab(ROW_SLABS[i]), row_slab(ROW_SLABS[HALF + i])
        out_ref[i * P_COV : (i + 1) * P_COV, :] = jnp.where(row <= column, upper, lower)
        out_ref[DIAG_ROW + i : DIAG_ROW + i + 1, :] = jnp.sum(
            jnp.where(row == column, lower, 0.0), axis=0, keepdims=True
        )
    mom = mom_ref[...]
    out_ref[MOMENT_ROW : MOMENT_ROW + N_BASIS, 0:P_COV] = mom[0:8, 0:P_COV] + mom[8:16, 0:P_COV] + mom[0:8, P_COV:]


def local_sums(count, covariates, intervals, offsets, responses):
    slots = covariates.shape[1]
    in_place = pl.BlockSpec(memory_space=pltpu.HBM)
    high = pltpu.VMEM((WIDTH + len(HI_SUMS) * P_COV, CHUNK), BF16)
    low = pltpu.VMEM((WIDTH + len(LO_SUMS) * P_COV, CHUNK), BF16)
    return pl.pallas_call(
        gram_kernel,
        in_specs=[pl.BlockSpec(memory_space=pltpu.SMEM), in_place, in_place, in_place, in_place],
        out_shape=jax.ShapeDtypeStruct((SLAB_ROWS, 128), F32),
        scratch_shapes=[
            pltpu.VMEM((P_COV, slots), F32),
            pltpu.VMEM((1, slots), jnp.int32),
            pltpu.VMEM((1, slots), F32),
            pltpu.VMEM((1, slots), F32),
            high,
            high,
            low,
            low,
            pltpu.VMEM((2 * len(MID_ROWS) * P_COV, 256), F32),
            pltpu.VMEM(((len(END_HI_ROWS) + len(END_LO_ROWS)) * P_COV, 256), F32),
            pltpu.VMEM((16, 128), F32),
            pltpu.SemaphoreType.DMA((3,)),
            pltpu.SemaphoreType.DMA((slots // (UNROLL * CHUNK),)),
        ],
        compiler_params=pltpu.CompilerParams(vmem_limit_bytes=62 * 1024 * 1024),
        name="local_sums",
    )(count, covariates, intervals[None, :], offsets[None, :], responses[None, :])


def sum_repeat_kernel(parts, copies, in_ref, out_ref):
    rows = in_ref.shape[0] // parts
    total = in_ref[0:rows, :]
    for i in range(1, parts):
        total = total + in_ref[i * rows : (i + 1) * rows, :]
    for i in range(copies):
        out_ref[i * rows : (i + 1) * rows, :] = total


def sum_repeat(received, parts, copies):
    rows = received.shape[0] // parts
    return pl.pallas_call(
        lambda a, b: sum_repeat_kernel(parts, copies, a, b),
        out_shape=jax.ShapeDtypeStruct((copies * rows, 128), F32),
        compiler_params=pltpu.CompilerParams(vmem_limit_bytes=4 * 1024 * 1024),
        name="sum_repeat",
    )(received)


def lane_spread(tile, lane):
    return jnp.take_along_axis(tile, jnp.full(tile.shape, lane, jnp.int32), axis=1)


def row_spread(tile, row):
    return jnp.broadcast_to(tile[row : row + 1, :], tile.shape)


def three_terms(value):
    high = value.astype(BF16)
    rest = value - high.astype(F32)
    middle = rest.astype(BF16)
    return high, middle, (rest - middle.astype(F32)).astype(BF16)


TERM_PAIRS = [(0, 0), (0, 1), (1, 0), (1, 1), (0, 2), (2, 0)]


def float_product(left_terms, right_terms, contract):
    left_axis, right_axis = contract
    return lax.dot_general(
        jnp.concatenate([left_terms[i] for i, _ in TERM_PAIRS], axis=left_axis),
        jnp.concatenate([right_terms[i] for _, i in TERM_PAIRS], axis=right_axis),
        (((left_axis,), (right_axis,)), ((), ())),
        preferred_element_type=F32,
    )


def factor_tile(work, side):
    blocks = len(work)
    lanes = lax.broadcasted_iota(jnp.int32, (8, 128), 1)
    subs = lax.broadcasted_iota(jnp.int32, (8, 128), 0)
    factor_rows, inverse_rows = [], []
    for k in range(blocks):
        if k == 0:
            columns = [lane_spread(work[0], t) for t in range(8)]
        if k + 1 < blocks:
            ahead = [lane_spread(work[k + 1], 8 * k + 8 + t) for t in range(8)]
        entry = {(s, t): row_spread(columns[t], s) for t in range(8) for s in range(t, 8)}
        rows = [row_spread(work[k], t) for t in range(8)]
        siderows = [row_spread(side[k], t) for t in range(8)]
        pivot = entry[0, 0]
        pivots, reciprocals, scale = [], [], {}
        for t in range(8):
            reciprocal = 1.0 / pivot
            pivots.append(pivot)
            reciprocals.append(reciprocal)
            if t + 1 < 8:
                pivot = entry[t + 1, t + 1] - (entry[t + 1, t] * entry[t + 1, t]) * reciprocal
            for s in range(t + 1, 8):
                scale[s, t] = entry[s, t] * reciprocal
            for s in range(t + 1, 8):
                for u in range(t + 1, s + 1):
                    if (s, u) != (t + 1, t + 1):
                        entry[s, u] = entry[s, u] - scale[s, t] * entry[u, t]
                rows[s] = rows[s] - scale[s, t] * rows[t]
                siderows[s] = siderows[s] - scale[s, t] * siderows[t]
        near = k + 3 if k % 2 else k + 4
        for b in range(k + 1, min(near, blocks)):
            c = [lane_spread(work[b], 8 * k + t) for t in range(8)]
            for t in range(8):
                for s in range(t + 1, 8):
                    c[s] = c[s] - scale[s, t] * c[t]
                weight = c[t] * reciprocals[t]
                work[b] = work[b] - weight * rows[t]
                side[b] = side[b] - weight * siderows[t]
                if b == k + 1:
                    ahead = [ahead[u] - weight * row_spread(c[t], u) for u in range(8)]
        if k + 1 < blocks:
            columns = ahead
        out, sideout = jnp.zeros((8, 128), F32), jnp.zeros((8, 128), F32)
        for t in range(8):
            root = lax.rsqrt(pivots[t])
            out = jnp.where(subs == t, rows[t] * root, out)
            sideout = jnp.where(subs == t, siderows[t] * root, sideout)
        factor_rows.append(jnp.where(lanes >= subs + 8 * k, out, 0.0))
        inverse_rows.append(jnp.where(lanes <= subs + 8 * k, sideout, 0.0))
        if k % 2 and near < blocks:
            upper = jnp.concatenate(factor_rows[k - 1 :], axis=0)
            both = jnp.concatenate([upper, jnp.concatenate(inverse_rows[k - 1 :], axis=0)], axis=1)
            change = float_product(three_terms(upper), three_terms(both), (0, 0))
            for b in range(near, blocks):
                work[b] = work[b] - change[8 * b : 8 * b + 8, :128]
                side[b] = side[b] - change[8 * b : 8 * b + 8, 128:]
    return factor_rows, inverse_rows


def factor_kernel(sums_ref, smooth_ref, factor_ref, proj_ref, half_ref, gram_ref, inv_ref):
    row, column, left = slab_masks()
    second = np.zeros((N_BASIS - 2, N_BASIS))
    for i in range(N_BASIS - 2):
        second[i, i : i + 3] = (1.0, -2.0, 1.0)
    penalty = second.T @ second
    smooth = jnp.where(row == column, jnp.concatenate([smooth_ref[...], smooth_ref[...]], axis=1), 0.0)
    slabs, place = {}, {}

    def keep(entry, value):
        w, j_left, j_right = entry
        scale = jnp.where(left, float(penalty[j_left, 2 * w]), float(penalty[j_right, 2 * w + 1]))
        slabs[entry] = value * (1.0 / TOTAL_LIVE) + smooth * scale
        place[j_left, 2 * w] = entry
        if j_right >= 2 * w + 1:
            place[j_right, 2 * w + 1] = entry

    for i in range(HALF):
        packed = sums_ref[i * P_COV : (i + 1) * P_COV, :]
        turned = jnp.concatenate([packed[:, :P_COV].T, packed[:, P_COV:].T], axis=1)
        keep(ROW_SLABS[i], jnp.where(row <= column, packed, turned))
        diagonal = jnp.broadcast_to(sums_ref[DIAG_ROW + i : DIAG_ROW + i + 1, :], (P_COV, 128))
        keep(ROW_SLABS[HALF + i], jnp.where(row == column, diagonal, jnp.where(row > column, packed, turned)))
    swapped = {}

    def in_half(j, k, half):
        pair = (max(j, k), min(j, k))
        if pair not in place:
            return None
        entry = place[pair]
        if pair[1] % 2 == half:
            return slabs[entry]
        if entry not in swapped:
            swapped[entry] = pltpu.roll(slabs[entry], P_COV, 1)
        return swapped[entry]

    nothing = jnp.zeros((P_COV, 128), F32)
    for j in range(N_BASIS):
        for w in range(4):
            first, second = in_half(j, 2 * w, 0), in_half(j, 2 * w + 1, 1)
            first, second = (nothing if first is None else first), (nothing if second is None else second)
            half_ref[w, pl.ds(j, P_COV, N_BASIS), :] = first if first is second else jnp.where(left, first, second)
    for w in range(4):
        for i in range(4):
            turned = half_ref[w, 128 * i : 128 * i + 128, :].T
            above = 16 * (i + 1)
            for k in (2 * w, 2 * w + 1):
                gram_ref[i, pl.ds(k, above, N_BASIS), :] = turned[(k - 2 * w) * P_COV : (k - 2 * w) * P_COV + above, :]
    moment = sums_ref[MOMENT_ROW : MOMENT_ROW + N_BASIS, 0:P_COV].T * (1.0 / math.sqrt(TOTAL_LIVE))
    for j in range(N_BASIS):
        gram_ref[4, pl.ds(j, P_COV, N_BASIS), :] = jnp.broadcast_to(moment[:, j : j + 1], (P_COV, 128))

    factor_ref[...] = jnp.zeros_like(factor_ref)
    lanes = lax.broadcasted_iota(jnp.int32, (8, 128), 1)
    subs = lax.broadcasted_iota(jnp.int32, (8, 128), 0)

    def panel(p, _):
        start = pl.multiple_of(p * 128, 128)
        work = [gram_ref[p, pl.ds(pl.multiple_of(start + 8 * b, 8), 8), :] for b in range(16)]
        side = [jnp.where(lanes == subs + 8 * b, 1.0, 0.0).astype(F32) for b in range(16)]
        factor_rows, inverse_rows = factor_tile(work, side)
        for b in range(16):
            inv_ref[8 * b : 8 * b + 8, :] = inverse_rows[b]
            factor_ref[pl.ds(pl.multiple_of(start + 8 * b, 8), 8), pl.ds(start, 128)] = factor_rows[b]

        for q in range(4):

            @pl.when(p == q)
            def _():
                mine = slice(128 * q, 128 * q + 128)
                right = jnp.concatenate([gram_ref[w, mine, :] for w in range(q + 1, 5)], axis=1)
                solved = float_product(three_terms(inv_ref[...]), three_terms(right), (1, 0))
                terms = three_terms(solved)
                for w in range(q + 1, 5):
                    part = solved[:, 128 * (w - q - 1) : 128 * (w - q)]
                    if w < 4:
                        factor_ref[mine, 128 * w : 128 * w + 128] = part
                    else:
                        gram_ref[w, mine, :] = part
                for i in range(q + 1, 4):
                    at = 128 * (i - q - 1)
                    change = float_product(
                        [term[:, at : at + 128] for term in terms], [term[:, at:] for term in terms], (0, 0)
                    )
                    for w in range(i, 5):
                        gram_ref[w, 128 * i : 128 * i + 128, :] -= change[:, 128 * (w - i) : 128 * (w - i) + 128]

        return 0

    lax.fori_loop(0, 4, panel, 0)
    diagonal_mask = lax.broadcasted_iota(jnp.int32, (128, 128), 0) == lax.broadcasted_iota(jnp.int32, (128, 128), 1)
    for p in range(4):
        tile = gram_ref[4, 128 * p : 128 * p + 128, :]
        proj_ref[:, 128 * p : 128 * p + 128] = jnp.sum(jnp.where(diagonal_mask, tile, 0.0), axis=0, keepdims=True)


def factorize(sums, smoothing):
    return pl.pallas_call(
        factor_kernel,
        out_shape=(
            jax.ShapeDtypeStruct((WIDTH, WIDTH), F32),
            jax.ShapeDtypeStruct((1, WIDTH), F32),
        ),
        scratch_shapes=[
            pltpu.VMEM((4, WIDTH, 128), F32),
            pltpu.VMEM((5, WIDTH, 128), F32),
            pltpu.VMEM((128, 128), F32),
        ],
        compiler_params=pltpu.CompilerParams(vmem_limit_bytes=40 * 1024 * 1024),
        name="factorize",
    )(sums, smoothing[None, :])


NEAR = ("zn", "yn", "core", "x")
FAR = ("zf", "yf")


def exchange(rows, axes, parts):
    return lax.all_to_all(rows.reshape(parts, -1, 128), axes, 0, 0, tiled=True).reshape(-1, 128)


def per_device(covariates, intervals, offsets, responses, counts, smoothing):
    sums = local_sums(counts, covariates, intervals, offsets, responses)
    shares = sum_repeat(exchange(sums, NEAR, SHARES), SHARES, 16)
    shares = sum_repeat(exchange(shares, FAR, 16), 16, SHARES)
    factor, projected = factorize(exchange(shares, NEAR, SHARES), smoothing)
    return factor, projected[0]


def solution(mesh):
    fine = Mesh(mesh.devices.reshape(4, 2, 4, 2, 2, 4), ("zf", "zn", "yf", "yn", "core", "x"))
    spread = fine.axis_names
    return jax.shard_map(
        per_device,
        mesh=fine,
        in_specs=(P(None, spread), P(spread), P(spread), P(spread), P(spread), P()),
        out_specs=(P(), P()),
        check_vma=False,
    )
```

```python
import math

import jax
import jax.numpy as jnp
import numpy as np
from jax import lax
from jax.experimental import pallas as pl
from jax.experimental.pallas import tpu as pltpu
from jax.sharding import Mesh, PartitionSpec as P

P_COV = 64
N_BASIS = 8
WIDTH = P_COV * N_BASIS
CHUNK = 2048
UNROLL = 2
TOTAL_LIVE = 2097152
F32 = jnp.float32
BF16 = jnp.bfloat16
HIGHEST = lax.Precision.HIGHEST

ROW_SLABS = [(0, 0, 4), (0, 1, 1), (0, 2, 2), (0, 3, 3), (1, 2, 6), (1, 3, 3), (1, 4, 4), (1, 5, 5)]
ROW_SLABS += [(2, 4, 4), (2, 5, 5), (2, 6, 6), (2, 7, 7), (3, 6, 6), (3, 7, 7)]
HALF = len(ROW_SLABS) // 2
SHARES = 32
SHARE_ROWS = 16
SLAB_ROWS = SHARES * SHARE_ROWS
DIAG_ROW = HALF * P_COV
MOMENT_ROW = DIAG_ROW + 8
NT = (((1,), (1,)), ((), ()))
TN = (((0,), (0,)), ((), ()))


HI_SUMS = [(0, 7), (0, 6), (1, 7)]
LO_SUMS = [(0, 7), (0, 5), (1, 6), (2, 7)]
MID_ROWS = [8, 1, 6, 2, 3, 4, 5]
MID_PLACE = {0: 0, 7: 0, 1: 1, 6: 2, 2: 3, 3: 4, 4: 5, 5: 6}
END_HI_ROWS = [9, 10]
END_LO_ROWS = [9, 10, 11, 3, 4]


def basis_rows(j):
    return slice(j * P_COV, (j + 1) * P_COV)


def slab_masks():
    row = lax.broadcasted_iota(jnp.int32, (P_COV, 128), 0)
    column = lax.broadcasted_iota(jnp.int32, (P_COV, 128), 1)
    return row, column % P_COV, column < P_COV


def gram_kernel(
    count_ref, cov_hbm, int_hbm, off_hbm, resp_hbm, out_ref,
    cov_ref, int_ref, off_ref, resp_ref, hi_even, hi_odd, lo_even, lo_odd, mid_ref, end_ref, mom_ref, row_sem, cov_sem,
):
    count = count_ref[0]
    chunks = cov_hbm.shape[1] // CHUNK

    def columns(c):
        return pl.ds(pl.multiple_of(c * CHUNK, CHUNK), CHUNK)

    row_copies = [
        pltpu.make_async_copy(source, target, row_sem.at[i])
        for i, (source, target) in enumerate([(int_hbm, int_ref), (off_hbm, off_ref), (resp_hbm, resp_ref)])
    ]
    groups = chunks // UNROLL

    def cov_copy(i):
        part = pl.ds(pl.multiple_of(i * UNROLL * CHUNK, UNROLL * CHUNK), UNROLL * CHUNK)
        return pltpu.make_async_copy(cov_hbm.at[:, part], cov_ref.at[:, part], cov_sem.at[i])

    for copy in row_copies:
        copy.start()
    for i in range(groups):
        cov_copy(i).start()
    mid_ref[...] = jnp.zeros_like(mid_ref)
    end_ref[...] = jnp.zeros_like(end_ref)
    mom_ref[...] = jnp.zeros_like(mom_ref)
    for copy in row_copies:
        copy.wait()

    def build(c, hi_ref, lo_ref):
        part = columns(c)
        cov = cov_ref[:, part]
        interval = int_ref[:, part]
        within = off_ref[:, part]
        slot = lax.broadcasted_iota(jnp.int32, (1, CHUNK), 1) + c * CHUNK
        live = jnp.where(slot < count, 1.0, 0.0).astype(F32)
        square = within * within
        cube = square * within
        rest = 1.0 - within
        first = rest * rest * rest * (1.0 / 6.0) * live
        second = (3.0 * cube - 6.0 * square + 4.0) * (1.0 / 6.0) * live
        third = (-3.0 * cube + 3.0 * square + 3.0 * within + 1.0) * (1.0 / 6.0) * live
        fourth = cube * (1.0 / 6.0) * live
        weights, highs, lows = [], [], []
        for j in range(N_BASIS):
            value = jnp.where(interval == j, first, 0.0)
            value = jnp.where(interval + 1 == j, second, value)
            value = jnp.where(interval + 2 == j, third, value)
            value = jnp.where(interval + 3 == j, fourth, value)
            weights.append(value)
            design = cov * value
            highs.append(design.astype(BF16))
            lows.append((design - highs[j].astype(F32)).astype(BF16))
            hi_ref[basis_rows(j), :] = highs[j]
            lo_ref[basis_rows(j), :] = lows[j]
        for i, (j, k) in enumerate(HI_SUMS):
            hi_ref[basis_rows(N_BASIS + i), :] = highs[j] + highs[k]
        for i, (j, k) in enumerate(LO_SUMS):
            lo_ref[basis_rows(N_BASIS + i), :] = lows[j] + lows[k]
        cov_high = cov.astype(BF16)
        cov_low = (cov - cov_high.astype(F32)).astype(BF16)
        weighted = jnp.concatenate(weights, axis=0) * resp_ref[:, part]
        weighted_high = weighted.astype(BF16)
        weighted_low = (weighted - weighted_high.astype(F32)).astype(BF16)
        mom_ref[...] += lax.dot_general(
            jnp.concatenate([weighted_high, weighted_low], axis=0),
            jnp.concatenate([cov_high, cov_low], axis=0),
            NT,
            preferred_element_type=F32,
        )

    def multiply(hi_ref, lo_ref):
        def rows_of(ref, places):
            return [ref[basis_rows(place), :] for place in places]

        middle = jnp.concatenate(rows_of(hi_ref, MID_ROWS) + rows_of(lo_ref, MID_ROWS), axis=0)
        mid_ref[...] += lax.dot_general(middle, hi_ref[128:384, :], NT, preferred_element_type=F32)
        ends = jnp.concatenate(rows_of(hi_ref, END_HI_ROWS) + rows_of(lo_ref, END_LO_ROWS), axis=0)
        across = jnp.concatenate([hi_ref[0:128, :], hi_ref[384:512, :]], axis=0)
        end_ref[...] += lax.dot_general(ends, across, NT, preferred_element_type=F32)

    def group(i, _):
        cov_copy(i).wait()
        for c in range(UNROLL):
            hi_ref, lo_ref = (hi_odd, lo_odd) if c % 2 else (hi_even, lo_even)
            build(UNROLL * i + c, hi_ref, lo_ref)
            multiply(hi_ref, lo_ref)
        return 0

    def unused(i, _):
        cov_copy(i).wait()
        return 0

    used = pl.cdiv(count, UNROLL * CHUNK)
    lax.fori_loop(0, used, group, 0)
    lax.fori_loop(used, groups, unused, 0)

    row, column, left = slab_masks()
    tiles = {}

    def high_rows(j, w):
        if w in (1, 2):
            return mid_ref[basis_rows(MID_PLACE[j]), 128 * w - 128 : 128 * w]
        return end_ref[basis_rows(j % 6), 0:128] if w == 0 else end_ref[basis_rows(j - 6), 128:256]

    def low_rows(j, w):
        if w in (1, 2):
            return mid_ref[basis_rows(len(MID_ROWS) + MID_PLACE[j]), 128 * w - 128 : 128 * w]
        place = len(END_HI_ROWS) + (j if j < 5 else j - 5)
        return end_ref[basis_rows(place), 0:128] if w == 0 else end_ref[basis_rows(place), 128:256]

    def tile(t, w):
        turn_high = w == 0 and t in (1, 2)
        straight = [low_rows(j, w) if turn_high else low_rows(j, w) + high_rows(j, w) for j in (2 * t, 2 * t + 1)]
        turned = [low_rows(k, t) + high_rows(k, t) if turn_high else low_rows(k, t) for k in (2 * w, 2 * w + 1)]
        return jnp.concatenate(straight, axis=0) + jnp.concatenate(turned, axis=0).T

    def row_slab(entry):
        w, j_left, j_right = entry
        pieces = []
        for j in (j_left, j_right):
            t = j // 2
            if (t, w) not in tiles:
                tiles[t, w] = tile(t, w)
            pieces.append(tiles[t, w][(j % 2) * P_COV : (j % 2 + 1) * P_COV, :])
        return pieces[0] if j_left == j_right else jnp.where(left, pieces[0], pieces[1])

    out_ref[DIAG_ROW:, :] = jnp.zeros((SLAB_ROWS - DIAG_ROW, 128), F32)
    for i in range(HALF):
        upper, lower = row_slab(ROW_SLABS[i]), row_slab(ROW_SLABS[HALF + i])
        out_ref[i * P_COV : (i + 1) * P_COV, :] = jnp.where(row <= column, upper, lower)
        out_ref[DIAG_ROW + i : DIAG_ROW + i + 1, :] = jnp.sum(
            jnp.where(row == column, lower, 0.0), axis=0, keepdims=True
        )
    mom = mom_ref[...]
    out_ref[MOMENT_ROW : MOMENT_ROW + N_BASIS, 0:P_COV] = mom[0:8, 0:P_COV] + mom[8:16, 0:P_COV] + mom[0:8, P_COV:]


def local_sums(count, covariates, intervals, offsets, responses):
    slots = covariates.shape[1]
    in_place = pl.BlockSpec(memory_space=pltpu.HBM)
    high = pltpu.VMEM((WIDTH + len(HI_SUMS) * P_COV, CHUNK), BF16)
    low = pltpu.VMEM((WIDTH + len(LO_SUMS) * P_COV, CHUNK), BF16)
    return pl.pallas_call(
        gram_kernel,
        in_specs=[pl.BlockSpec(memory_space=pltpu.SMEM), in_place, in_place, in_place, in_place],
        out_shape=jax.ShapeDtypeStruct((SLAB_ROWS, 128), F32),
        scratch_shapes=[
            pltpu.VMEM((P_COV, slots), F32),
            pltpu.VMEM((1, slots), jnp.int32),
            pltpu.VMEM((1, slots), F32),
            pltpu.VMEM((1, slots), F32),
            high,
            high,
            low,
            low,
            pltpu.VMEM((2 * len(MID_ROWS) * P_COV, 256), F32),
            pltpu.VMEM(((len(END_HI_ROWS) + len(END_LO_ROWS)) * P_COV, 256), F32),
            pltpu.VMEM((16, 128), F32),
            pltpu.SemaphoreType.DMA((3,)),
            pltpu.SemaphoreType.DMA((slots // (UNROLL * CHUNK),)),
        ],
        compiler_params=pltpu.CompilerParams(vmem_limit_bytes=62 * 1024 * 1024),
        name="local_sums",
    )(count, covariates, intervals[None, :], offsets[None, :], responses[None, :])


def sum_repeat_kernel(parts, copies, in_ref, out_ref):
    rows = in_ref.shape[0] // parts
    total = in_ref[0:rows, :]
    for i in range(1, parts):
        total = total + in_ref[i * rows : (i + 1) * rows, :]
    for i in range(copies):
        out_ref[i * rows : (i + 1) * rows, :] = total


def sum_repeat(received, parts, copies):
    rows = received.shape[0] // parts
    return pl.pallas_call(
        lambda a, b: sum_repeat_kernel(parts, copies, a, b),
        out_shape=jax.ShapeDtypeStruct((copies * rows, 128), F32),
        compiler_params=pltpu.CompilerParams(vmem_limit_bytes=4 * 1024 * 1024),
        name="sum_repeat",
    )(received)


def lane_spread(tile, lane):
    return jnp.take_along_axis(tile, jnp.full(tile.shape, lane, jnp.int32), axis=1)


def row_spread(tile, row):
    return jnp.broadcast_to(tile[row : row + 1, :], tile.shape)


def three_terms(value):
    high = value.astype(BF16)
    rest = value - high.astype(F32)
    middle = rest.astype(BF16)
    return high, middle, (rest - middle.astype(F32)).astype(BF16)


TERM_PAIRS = [(0, 0), (0, 1), (1, 0), (1, 1), (0, 2), (2, 0)]


def float_product(left_terms, right_terms, contract):
    left_axis, right_axis = contract
    return lax.dot_general(
        jnp.concatenate([left_terms[i] for i, _ in TERM_PAIRS], axis=left_axis),
        jnp.concatenate([right_terms[i] for _, i in TERM_PAIRS], axis=right_axis),
        (((left_axis,), (right_axis,)), ((), ())),
        preferred_element_type=F32,
    )


def factor_tile(work, side, side_is_identity):
    blocks = len(work)
    lanes = lax.broadcasted_iota(jnp.int32, (8, 128), 1)
    subs = lax.broadcasted_iota(jnp.int32, (8, 128), 0)
    factor_rows, solved_rows = [], []
    for k in range(blocks):
        if k == 0:
            columns = [lane_spread(work[0], t) for t in range(8)]
        if k + 1 < blocks:
            ahead = [lane_spread(work[k + 1], 8 * k + 8 + t) for t in range(8)]
        entry = {(s, t): row_spread(columns[t], s) for t in range(8) for s in range(t, 8)}
        rows = [row_spread(work[k], t) for t in range(8)]
        siderows = [row_spread(side[k], t) for t in range(8)]
        pivot = entry[0, 0]
        pivots, reciprocals, scale = [], [], {}
        for t in range(8):
            reciprocal = 1.0 / pivot
            pivots.append(pivot)
            reciprocals.append(reciprocal)
            if t + 1 < 8:
                pivot = entry[t + 1, t + 1] - (entry[t + 1, t] * entry[t + 1, t]) * reciprocal
            for s in range(t + 1, 8):
                scale[s, t] = entry[s, t] * reciprocal
            for s in range(t + 1, 8):
                for u in range(t + 1, s + 1):
                    if (s, u) != (t + 1, t + 1):
                        entry[s, u] = entry[s, u] - scale[s, t] * entry[u, t]
                rows[s] = rows[s] - scale[s, t] * rows[t]
                siderows[s] = siderows[s] - scale[s, t] * siderows[t]
        near = k + 3 if k % 2 else k + 4
        for b in range(k + 1, min(near, blocks)):
            c = [lane_spread(work[b], 8 * k + t) for t in range(8)]
            for t in range(8):
                for s in range(t + 1, 8):
                    c[s] = c[s] - scale[s, t] * c[t]
                weight = c[t] * reciprocals[t]
                work[b] = work[b] - weight * rows[t]
                side[b] = side[b] - weight * siderows[t]
                if b == k + 1:
                    ahead = [ahead[u] - weight * row_spread(c[t], u) for u in range(8)]
        if k + 1 < blocks:
            columns = ahead
        out, sideout = jnp.zeros((8, 128), F32), jnp.zeros((8, 128), F32)
        for t in range(8):
            root = lax.rsqrt(pivots[t])
            out = jnp.where(subs == t, rows[t] * root, out)
            sideout = jnp.where(subs == t, siderows[t] * root, sideout)
        factor_rows.append(jnp.where(lanes >= subs + 8 * k, out, 0.0))
        solved_rows.append(jnp.where(lanes <= subs + 8 * k, sideout, 0.0) if side_is_identity else sideout)
        if k % 2 and near < blocks:
            upper = jnp.concatenate(factor_rows[k - 1 :], axis=0)
            both = jnp.concatenate([upper, jnp.concatenate(solved_rows[k - 1 :], axis=0)], axis=1)
            change = float_product(three_terms(upper), three_terms(both), (0, 0))
            for b in range(near, blocks):
                work[b] = work[b] - change[8 * b : 8 * b + 8, :128]
                side[b] = side[b] - change[8 * b : 8 * b + 8, 128:]
    return factor_rows, solved_rows


def factor_kernel(sums_ref, smooth_ref, factor_ref, proj_ref, half_ref, gram_ref):
    row, column, left = slab_masks()
    second = np.zeros((N_BASIS - 2, N_BASIS))
    for i in range(N_BASIS - 2):
        second[i, i : i + 3] = (1.0, -2.0, 1.0)
    penalty = second.T @ second
    smooth = jnp.where(row == column, jnp.concatenate([smooth_ref[...], smooth_ref[...]], axis=1), 0.0)
    diagonals = sums_ref[DIAG_ROW : DIAG_ROW + 8, :]
    diagonals = (diagonals, pltpu.roll(diagonals, P_COV, 1))
    packed, turned = {}, {}
    for i in range(0, HALF, 2):
        both = sums_ref[i * P_COV : (i + 2) * P_COV, :]
        top, bottom = both.T[:P_COV], both.T[P_COV:]
        top_moved, bottom_moved = pltpu.roll(top, P_COV, 1), pltpu.roll(bottom, P_COV, 1)
        packed[i], packed[i + 1] = both[:P_COV], both[P_COV:]
        turned[i, 0] = jnp.where(left, top, bottom_moved)
        turned[i, 1] = jnp.where(left, bottom, top_moved)
        turned[i + 1, 0] = jnp.where(left, top_moved, bottom)
        turned[i + 1, 1] = jnp.where(left, bottom_moved, top)
    place, slabs = {}, {}
    for number, (w, j_left, j_right) in enumerate(ROW_SLABS):
        place[j_left, 2 * w] = number
        if j_right >= 2 * w + 1:
            place[j_right, 2 * w + 1] = number

    def slab(number, swap):
        if (number, swap) not in slabs:
            i = number % HALF
            straight = pltpu.roll(packed[i], P_COV, 1) if swap else packed[i]
            if number < HALF:
                value = jnp.where(row <= column, straight, turned[i, swap])
            else:
                diagonal = jnp.broadcast_to(diagonals[swap][i : i + 1, :], (P_COV, 128))
                value = jnp.where(row > column, straight, turned[i, swap])
                value = jnp.where(row == column, diagonal, value)
            w, j_left, j_right = ROW_SLABS[number]
            factors = (float(penalty[j_left, 2 * w]), float(penalty[j_right, 2 * w + 1]))
            scale = jnp.where(left, factors[swap], factors[1 - swap])
            slabs[number, swap] = value * (1.0 / TOTAL_LIVE) + smooth * scale
        return slabs[number, swap]

    def in_half(j, k, half):
        pair = (max(j, k), min(j, k))
        return slab(place[pair], int(pair[1] % 2 != half)) if pair in place else None

    nothing = jnp.zeros((P_COV, 128), F32)
    for j in range(N_BASIS):
        for w in range(4):
            first, second = in_half(j, 2 * w, 0), in_half(j, 2 * w + 1, 1)
            first, second = (nothing if first is None else first), (nothing if second is None else second)
            half_ref[w, pl.ds(j, P_COV, N_BASIS), :] = first if first is second else jnp.where(left, first, second)
    for w in range(4):
        for i in range(4):
            turned = half_ref[w, 128 * i : 128 * i + 128, :].T
            above = 16 * (i + 1)
            for k in (2 * w, 2 * w + 1):
                gram_ref[i, pl.ds(k, above, N_BASIS), :] = turned[(k - 2 * w) * P_COV : (k - 2 * w) * P_COV + above, :]
    moment = sums_ref[MOMENT_ROW : MOMENT_ROW + N_BASIS, 0:P_COV].T * (1.0 / math.sqrt(TOTAL_LIVE))
    for j in range(N_BASIS):
        gram_ref[4, pl.ds(j, P_COV, N_BASIS), :] = jnp.broadcast_to(moment[:, j : j + 1], (P_COV, 128))

    factor_ref[...] = jnp.zeros_like(factor_ref)
    lanes = lax.broadcasted_iota(jnp.int32, (8, 128), 1)
    subs = lax.broadcasted_iota(jnp.int32, (8, 128), 0)

    for p in range(4):
        mine = slice(128 * p, 128 * p + 128)
        work = [gram_ref[p, 128 * p + 8 * b : 128 * p + 8 * b + 8, :] for b in range(16)]
        last = p == 3
        if last:
            side = [gram_ref[4, 128 * p + 8 * b : 128 * p + 8 * b + 8, :] for b in range(16)]
        else:
            side = [jnp.where(lanes == subs + 8 * b, 1.0, 0.0).astype(F32) for b in range(16)]
        factor_rows, solved_rows = factor_tile(work, side, not last)
        factor_ref[mine, mine] = jnp.concatenate(factor_rows, axis=0)
        if last:
            gram_ref[4, mine, :] = jnp.concatenate(solved_rows, axis=0)
            break
        inverse = jnp.concatenate(solved_rows, axis=0)
        right = jnp.concatenate([gram_ref[w, mine, :] for w in range(p + 1, 5)], axis=1)
        solved = float_product(three_terms(inverse), three_terms(right), (1, 0))
        terms = three_terms(solved)
        for w in range(p + 1, 5):
            part = solved[:, 128 * (w - p - 1) : 128 * (w - p)]
            if w < 4:
                factor_ref[mine, 128 * w : 128 * w + 128] = part
            else:
                gram_ref[w, mine, :] = part
        for i in range(p + 1, 4):
            at = 128 * (i - p - 1)
            change = float_product([term[:, at : at + 128] for term in terms], [term[:, at:] for term in terms], (0, 0))
            for w in range(i, 5):
                gram_ref[w, 128 * i : 128 * i + 128, :] -= change[:, 128 * (w - i) : 128 * (w - i) + 128]
    diagonal_mask = lax.broadcasted_iota(jnp.int32, (128, 128), 0) == lax.broadcasted_iota(jnp.int32, (128, 128), 1)
    for p in range(4):
        tile = gram_ref[4, 128 * p : 128 * p + 128, :]
        proj_ref[:, 128 * p : 128 * p + 128] = jnp.sum(jnp.where(diagonal_mask, tile, 0.0), axis=0, keepdims=True)


def factorize(sums, smoothing):
    return pl.pallas_call(
        factor_kernel,
        out_shape=(
            jax.ShapeDtypeStruct((WIDTH, WIDTH), F32),
            jax.ShapeDtypeStruct((1, WIDTH), F32),
        ),
        scratch_shapes=[
            pltpu.VMEM((4, WIDTH, 128), F32),
            pltpu.VMEM((5, WIDTH, 128), F32),
        ],
        compiler_params=pltpu.CompilerParams(vmem_limit_bytes=40 * 1024 * 1024),
        name="factorize",
    )(sums, smoothing[None, :])


NEAR = ("zn", "yn", "core", "x")
FAR = ("zf", "yf")


def exchange(rows, axes, parts):
    return lax.all_to_all(rows.reshape(parts, -1, 128), axes, 0, 0, tiled=True).reshape(-1, 128)


def per_device(covariates, intervals, offsets, responses, counts, smoothing):
    sums = local_sums(counts, covariates, intervals, offsets, responses)
    shares = sum_repeat(exchange(sums, NEAR, SHARES), SHARES, 16)
    shares = sum_repeat(exchange(shares, FAR, 16), 16, SHARES)
    factor, projected = factorize(exchange(shares, NEAR, SHARES), smoothing)
    return factor, projected[0]


def solution(mesh):
    fine = Mesh(mesh.devices.reshape(4, 2, 4, 2, 2, 4), ("zf", "zn", "yf", "yn", "core", "x"))
    spread = fine.axis_names
    return jax.shard_map(
        per_device,
        mesh=fine,
        in_specs=(P(None, spread), P(spread), P(spread), P(spread), P(spread), P()),
        out_specs=(P(), P()),
        check_vma=False,
    )
```

```python
import math

import jax
import jax.numpy as jnp
import numpy as np
from jax import lax
from jax.experimental import pallas as pl
from jax.experimental.pallas import tpu as pltpu
from jax.sharding import Mesh, PartitionSpec as P

P_COV = 64
N_BASIS = 8
WIDTH = P_COV * N_BASIS
CHUNK = 2048
UNROLL = 2
TOTAL_LIVE = 2097152
F32 = jnp.float32
BF16 = jnp.bfloat16
HIGHEST = lax.Precision.HIGHEST

ROW_SLABS = [(0, 0, 4), (0, 1, 1), (0, 2, 2), (0, 3, 3), (1, 2, 6), (1, 3, 3), (1, 4, 4), (1, 5, 5)]
ROW_SLABS += [(2, 4, 4), (2, 5, 5), (2, 6, 6), (2, 7, 7), (3, 6, 6), (3, 7, 7)]
HALF = len(ROW_SLABS) // 2
SHARES = 32
SHARE_ROWS = 16
SLAB_ROWS = SHARES * SHARE_ROWS
NT = (((1,), (1,)), ((), ()))
TN = (((0,), (0,)), ((), ()))


HI_SUMS = [(0, 7), (0, 6), (1, 7)]
LO_SUMS = [(0, 7), (0, 5), (1, 6), (2, 7)]
MID_ROWS = [8, 1, 6, 2, 3, 4, 5]
MID_PLACE = {0: 0, 7: 0, 1: 1, 6: 2, 2: 3, 3: 4, 4: 5, 5: 6}
END_HI_ROWS = [9, 10]
END_LO_ROWS = [9, 10, 11, 3, 4]


def basis_rows(j):
    return slice(j * P_COV, (j + 1) * P_COV)


def turn(far):
    return 1 - ((far + 1) // 2) % 2


def block_rows(i):
    exchanged = 4 * turn(lax.axis_index("zf")) + 2 * turn(lax.axis_index("yf"))
    return pl.ds(pl.multiple_of(jnp.bitwise_xor(jnp.int32(i), exchanged) * P_COV, P_COV), P_COV)


def slab_masks():
    row = lax.broadcasted_iota(jnp.int32, (P_COV, 128), 0)
    column = lax.broadcasted_iota(jnp.int32, (P_COV, 128), 1)
    return row, column % P_COV, column < P_COV


def gram_kernel(
    count_ref, cov_hbm, int_hbm, off_hbm, resp_hbm, out_ref,
    cov_ref, int_ref, off_ref, resp_ref, hi_even, hi_odd, lo_even, lo_odd, mid_ref, end_ref, mom_ref, row_sem, cov_sem,
):
    count = count_ref[0]
    chunks = cov_hbm.shape[1] // CHUNK

    def columns(c):
        return pl.ds(pl.multiple_of(c * CHUNK, CHUNK), CHUNK)

    row_copies = [
        pltpu.make_async_copy(source, target, row_sem.at[i])
        for i, (source, target) in enumerate([(int_hbm, int_ref), (off_hbm, off_ref), (resp_hbm, resp_ref)])
    ]
    groups = chunks // UNROLL

    def cov_copy(i):
        part = pl.ds(pl.multiple_of(i * UNROLL * CHUNK, UNROLL * CHUNK), UNROLL * CHUNK)
        return pltpu.make_async_copy(cov_hbm.at[:, part], cov_ref.at[:, part], cov_sem.at[i])

    for copy in row_copies:
        copy.start()
    for i in range(groups):
        cov_copy(i).start()
    mid_ref[...] = jnp.zeros_like(mid_ref)
    end_ref[...] = jnp.zeros_like(end_ref)
    mom_ref[...] = jnp.zeros_like(mom_ref)
    for copy in row_copies:
        copy.wait()

    def build(c, hi_ref, lo_ref):
        part = columns(c)
        cov = cov_ref[:, part]
        interval = int_ref[:, part]
        within = off_ref[:, part]
        slot = lax.broadcasted_iota(jnp.int32, (1, CHUNK), 1) + c * CHUNK
        live = jnp.where(slot < count, 1.0, 0.0).astype(F32)
        square = within * within
        cube = square * within
        rest = 1.0 - within
        first = rest * rest * rest * (1.0 / 6.0) * live
        second = (3.0 * cube - 6.0 * square + 4.0) * (1.0 / 6.0) * live
        third = (-3.0 * cube + 3.0 * square + 3.0 * within + 1.0) * (1.0 / 6.0) * live
        fourth = cube * (1.0 / 6.0) * live
        weights, highs, lows = [], [], []
        for j in range(N_BASIS):
            value = jnp.where(interval == j, first, 0.0)
            value = jnp.where(interval + 1 == j, second, value)
            value = jnp.where(interval + 2 == j, third, value)
            value = jnp.where(interval + 3 == j, fourth, value)
            weights.append(value)
            design = cov * value
            highs.append(design.astype(BF16))
            lows.append((design - highs[j].astype(F32)).astype(BF16))
            hi_ref[basis_rows(j), :] = highs[j]
            lo_ref[basis_rows(j), :] = lows[j]
        for i, (j, k) in enumerate(HI_SUMS):
            hi_ref[basis_rows(N_BASIS + i), :] = highs[j] + highs[k]
        for i, (j, k) in enumerate(LO_SUMS):
            lo_ref[basis_rows(N_BASIS + i), :] = lows[j] + lows[k]
        cov_high = cov.astype(BF16)
        cov_low = (cov - cov_high.astype(F32)).astype(BF16)
        weighted = jnp.concatenate(weights, axis=0) * resp_ref[:, part]
        weighted_high = weighted.astype(BF16)
        weighted_low = (weighted - weighted_high.astype(F32)).astype(BF16)
        mom_ref[...] += lax.dot_general(
            jnp.concatenate([weighted_high, weighted_low], axis=0),
            jnp.concatenate([cov_high, cov_low], axis=0),
            NT,
            preferred_element_type=F32,
        )

    def multiply(hi_ref, lo_ref):
        def rows_of(ref, places):
            return [ref[basis_rows(place), :] for place in places]

        middle = jnp.concatenate(rows_of(hi_ref, MID_ROWS) + rows_of(lo_ref, MID_ROWS), axis=0)
        mid_ref[...] += lax.dot_general(middle, hi_ref[128:384, :], NT, preferred_element_type=F32)
        ends = jnp.concatenate(rows_of(hi_ref, END_HI_ROWS) + rows_of(lo_ref, END_LO_ROWS), axis=0)
        across = jnp.concatenate([hi_ref[0:128, :], hi_ref[384:512, :]], axis=0)
        end_ref[...] += lax.dot_general(ends, across, NT, preferred_element_type=F32)

    def group(i, _):
        cov_copy(i).wait()
        for c in range(UNROLL):
            hi_ref, lo_ref = (hi_odd, lo_odd) if c % 2 else (hi_even, lo_even)
            build(UNROLL * i + c, hi_ref, lo_ref)
            multiply(hi_ref, lo_ref)
        return 0

    def unused(i, _):
        cov_copy(i).wait()
        return 0

    used = pl.cdiv(count, UNROLL * CHUNK)
    lax.fori_loop(0, used, group, 0)
    lax.fori_loop(used, groups, unused, 0)

    row, column, left = slab_masks()
    tiles = {}

    def high_rows(j, w):
        if w in (1, 2):
            return mid_ref[basis_rows(MID_PLACE[j]), 128 * w - 128 : 128 * w]
        return end_ref[basis_rows(j % 6), 0:128] if w == 0 else end_ref[basis_rows(j - 6), 128:256]

    def low_rows(j, w):
        if w in (1, 2):
            return mid_ref[basis_rows(len(MID_ROWS) + MID_PLACE[j]), 128 * w - 128 : 128 * w]
        place = len(END_HI_ROWS) + (j if j < 5 else j - 5)
        return end_ref[basis_rows(place), 0:128] if w == 0 else end_ref[basis_rows(place), 128:256]

    def tile(t, w):
        turn_high = w == 0 and t in (1, 2)
        straight = [low_rows(j, w) if turn_high else low_rows(j, w) + high_rows(j, w) for j in (2 * t, 2 * t + 1)]
        turned = [low_rows(k, t) + high_rows(k, t) if turn_high else low_rows(k, t) for k in (2 * w, 2 * w + 1)]
        return jnp.concatenate(straight, axis=0) + jnp.concatenate(turned, axis=0).T

    def row_slab(entry):
        w, j_left, j_right = entry
        pieces = []
        for j in (j_left, j_right):
            t = j // 2
            if (t, w) not in tiles:
                tiles[t, w] = tile(t, w)
            pieces.append(tiles[t, w][(j % 2) * P_COV : (j % 2 + 1) * P_COV, :])
        return pieces[0] if j_left == j_right else jnp.where(left, pieces[0], pieces[1])

    small = [jnp.zeros((P_COV, 128), F32)]
    for i in range(HALF):
        upper, lower = row_slab(ROW_SLABS[i]), row_slab(ROW_SLABS[HALF + i])
        out_ref[block_rows(i), :] = jnp.where(row <= column, upper, lower)
        diagonal = jnp.sum(jnp.where(row == column, lower, 0.0), axis=0, keepdims=True)
        small.append(jnp.where(row == i, diagonal, small[-1]))
    mom = mom_ref[...]
    moment = mom[0:8, :] + mom[8:16, :] + pltpu.roll(mom[0:8, :], P_COV, 1)
    out_ref[block_rows(HALF), :] = jnp.concatenate([small[-1][0:8], moment, small[-1][16:]], axis=0)


def local_sums(count, covariates, intervals, offsets, responses):
    slots = covariates.shape[1]
    in_place = pl.BlockSpec(memory_space=pltpu.HBM)
    high = pltpu.VMEM((WIDTH + len(HI_SUMS) * P_COV, CHUNK), BF16)
    low = pltpu.VMEM((WIDTH + len(LO_SUMS) * P_COV, CHUNK), BF16)
    return pl.pallas_call(
        gram_kernel,
        in_specs=[pl.BlockSpec(memory_space=pltpu.SMEM), in_place, in_place, in_place, in_place],
        out_shape=jax.ShapeDtypeStruct((SLAB_ROWS, 128), F32),
        scratch_shapes=[
            pltpu.VMEM((P_COV, slots), F32),
            pltpu.VMEM((1, slots), jnp.int32),
            pltpu.VMEM((1, slots), F32),
            pltpu.VMEM((1, slots), F32),
            high,
            high,
            low,
            low,
            pltpu.VMEM((2 * len(MID_ROWS) * P_COV, 256), F32),
            pltpu.VMEM(((len(END_HI_ROWS) + len(END_LO_ROWS)) * P_COV, 256), F32),
            pltpu.VMEM((16, 128), F32),
            pltpu.SemaphoreType.DMA((3,)),
            pltpu.SemaphoreType.DMA((slots // (UNROLL * CHUNK),)),
        ],
        compiler_params=pltpu.CompilerParams(vmem_limit_bytes=62 * 1024 * 1024),
        name="local_sums",
    )(count, covariates, intervals[None, :], offsets[None, :], responses[None, :])


def sum_repeat_kernel(parts, copies, in_ref, out_ref):
    rows = in_ref.shape[0] // parts
    total = in_ref[0:rows, :]
    for i in range(1, parts):
        total = total + in_ref[i * rows : (i + 1) * rows, :]
    for i in range(copies):
        out_ref[i * rows : (i + 1) * rows, :] = total


def sum_repeat(received, parts, copies):
    rows = received.shape[0] // parts
    return pl.pallas_call(
        lambda a, b: sum_repeat_kernel(parts, copies, a, b),
        out_shape=jax.ShapeDtypeStruct((copies * rows, 128), F32),
        compiler_params=pltpu.CompilerParams(vmem_limit_bytes=4 * 1024 * 1024),
        name="sum_repeat",
    )(received)


def lane_spread(tile, lane):
    return jnp.take_along_axis(tile, jnp.full(tile.shape, lane, jnp.int32), axis=1)


def row_spread(tile, row):
    return jnp.broadcast_to(tile[row : row + 1, :], tile.shape)


def three_terms(value):
    high = value.astype(BF16)
    rest = value - high.astype(F32)
    middle = rest.astype(BF16)
    return high, middle, (rest - middle.astype(F32)).astype(BF16)


TERM_PAIRS = [(0, 0), (0, 1), (1, 0), (1, 1), (0, 2), (2, 0)]


def float_product(left_terms, right_terms, contract):
    left_axis, right_axis = contract
    return lax.dot_general(
        jnp.concatenate([left_terms[i] for i, _ in TERM_PAIRS], axis=left_axis),
        jnp.concatenate([right_terms[i] for _, i in TERM_PAIRS], axis=right_axis),
        (((left_axis,), (right_axis,)), ((), ())),
        preferred_element_type=F32,
    )


def factor_tile(work, side, side_is_identity):
    blocks = len(work)
    lanes = lax.broadcasted_iota(jnp.int32, (8, 128), 1)
    subs = lax.broadcasted_iota(jnp.int32, (8, 128), 0)
    factor_rows, solved_rows = [], []
    for k in range(blocks):
        if k == 0:
            columns = [lane_spread(work[0], t) for t in range(8)]
        if k + 1 < blocks:
            ahead = [lane_spread(work[k + 1], 8 * k + 8 + t) for t in range(8)]
        entry = {(s, t): row_spread(columns[t], s) for t in range(8) for s in range(t, 8)}
        rows = [row_spread(work[k], t) for t in range(8)]
        siderows = [row_spread(side[k], t) for t in range(8)]
        pivot = entry[0, 0]
        pivots, reciprocals, scale = [], [], {}
        for t in range(8):
            reciprocal = 1.0 / pivot
            pivots.append(pivot)
            reciprocals.append(reciprocal)
            if t + 1 < 8:
                pivot = entry[t + 1, t + 1] - (entry[t + 1, t] * entry[t + 1, t]) * reciprocal
            for s in range(t + 1, 8):
                scale[s, t] = entry[s, t] * reciprocal
            for s in range(t + 1, 8):
                for u in range(t + 1, s + 1):
                    if (s, u) != (t + 1, t + 1):
                        entry[s, u] = entry[s, u] - scale[s, t] * entry[u, t]
                rows[s] = rows[s] - scale[s, t] * rows[t]
                siderows[s] = siderows[s] - scale[s, t] * siderows[t]
        near = k + 3 if k % 2 else k + 4
        for b in range(k + 1, min(near, blocks)):
            c = [lane_spread(work[b], 8 * k + t) for t in range(8)]
            for t in range(8):
                for s in range(t + 1, 8):
                    c[s] = c[s] - scale[s, t] * c[t]
                weight = c[t] * reciprocals[t]
                work[b] = work[b] - weight * rows[t]
                side[b] = side[b] - weight * siderows[t]
                if b == k + 1:
                    ahead = [ahead[u] - weight * row_spread(c[t], u) for u in range(8)]
        if k + 1 < blocks:
            columns = ahead
        out, sideout = jnp.zeros((8, 128), F32), jnp.zeros((8, 128), F32)
        for t in range(8):
            root = lax.rsqrt(pivots[t])
            out = jnp.where(subs == t, rows[t] * root, out)
            sideout = jnp.where(subs == t, siderows[t] * root, sideout)
        factor_rows.append(jnp.where(lanes >= subs + 8 * k, out, 0.0))
        solved_rows.append(jnp.where(lanes <= subs + 8 * k, sideout, 0.0) if side_is_identity else sideout)
        if k % 2 and near < blocks:
            upper = jnp.concatenate(factor_rows[k - 1 :], axis=0)
            both = jnp.concatenate([upper, jnp.concatenate(solved_rows[k - 1 :], axis=0)], axis=1)
            change = float_product(three_terms(upper), three_terms(both), (0, 0))
            for b in range(near, blocks):
                work[b] = work[b] - change[8 * b : 8 * b + 8, :128]
                side[b] = side[b] - change[8 * b : 8 * b + 8, 128:]
    return factor_rows, solved_rows


def factor_kernel(sums_ref, smooth_ref, factor_ref, proj_ref, half_ref, gram_ref):
    row, column, left = slab_masks()
    second = np.zeros((N_BASIS - 2, N_BASIS))
    for i in range(N_BASIS - 2):
        second[i, i : i + 3] = (1.0, -2.0, 1.0)
    penalty = second.T @ second
    smooth = jnp.where(row == column, jnp.concatenate([smooth_ref[...], smooth_ref[...]], axis=1), 0.0)
    small = sums_ref[block_rows(HALF), :]
    diagonals = small[0:8]
    diagonals = (diagonals, pltpu.roll(diagonals, P_COV, 1))
    packed, turned = {}, {}
    for i in range(0, HALF, 2):
        both = jnp.concatenate([sums_ref[block_rows(i), :], sums_ref[block_rows(i + 1), :]], axis=0)
        top, bottom = both.T[:P_COV], both.T[P_COV:]
        top_moved, bottom_moved = pltpu.roll(top, P_COV, 1), pltpu.roll(bottom, P_COV, 1)
        packed[i], packed[i + 1] = both[:P_COV], both[P_COV:]
        turned[i, 0] = jnp.where(left, top, bottom_moved)
        turned[i, 1] = jnp.where(left, bottom, top_moved)
        turned[i + 1, 0] = jnp.where(left, top_moved, bottom)
        turned[i + 1, 1] = jnp.where(left, bottom_moved, top)
    place, slabs = {}, {}
    for number, (w, j_left, j_right) in enumerate(ROW_SLABS):
        place[j_left, 2 * w] = number
        if j_right >= 2 * w + 1:
            place[j_right, 2 * w + 1] = number

    def slab(number, swap):
        if (number, swap) not in slabs:
            i = number % HALF
            straight = pltpu.roll(packed[i], P_COV, 1) if swap else packed[i]
            if number < HALF:
                value = jnp.where(row <= column, straight, turned[i, swap])
            else:
                diagonal = jnp.broadcast_to(diagonals[swap][i : i + 1, :], (P_COV, 128))
                value = jnp.where(row > column, straight, turned[i, swap])
                value = jnp.where(row == column, diagonal, value)
            w, j_left, j_right = ROW_SLABS[number]
            factors = (float(penalty[j_left, 2 * w]), float(penalty[j_right, 2 * w + 1]))
            scale = jnp.where(left, factors[swap], factors[1 - swap])
            slabs[number, swap] = value * (1.0 / TOTAL_LIVE) + smooth * scale
        return slabs[number, swap]

    def in_half(j, k, half):
        pair = (max(j, k), min(j, k))
        return slab(place[pair], int(pair[1] % 2 != half)) if pair in place else None

    nothing = jnp.zeros((P_COV, 128), F32)
    for j in range(N_BASIS):
        for w in range(4):
            first, second = in_half(j, 2 * w, 0), in_half(j, 2 * w + 1, 1)
            first, second = (nothing if first is None else first), (nothing if second is None else second)
            half_ref[w, pl.ds(j, P_COV, N_BASIS), :] = first if first is second else jnp.where(left, first, second)
    for w in range(4):
        for i in range(4):
            turned = half_ref[w, 128 * i : 128 * i + 128, :].T
            above = 16 * (i + 1)
            for k in (2 * w, 2 * w + 1):
                gram_ref[i, pl.ds(k, above, N_BASIS), :] = turned[(k - 2 * w) * P_COV : (k - 2 * w) * P_COV + above, :]
    moment = small[8:16, 0:P_COV].T * (1.0 / math.sqrt(TOTAL_LIVE))
    for j in range(N_BASIS):
        gram_ref[4, pl.ds(j, P_COV, N_BASIS), :] = jnp.broadcast_to(moment[:, j : j + 1], (P_COV, 128))

    factor_ref[...] = jnp.zeros_like(factor_ref)
    lanes = lax.broadcasted_iota(jnp.int32, (8, 128), 1)
    subs = lax.broadcasted_iota(jnp.int32, (8, 128), 0)

    for p in range(4):
        mine = slice(128 * p, 128 * p + 128)
        work = [gram_ref[p, 128 * p + 8 * b : 128 * p + 8 * b + 8, :] for b in range(16)]
        last = p == 3
        if last:
            side = [gram_ref[4, 128 * p + 8 * b : 128 * p + 8 * b + 8, :] for b in range(16)]
        else:
            side = [jnp.where(lanes == subs + 8 * b, 1.0, 0.0).astype(F32) for b in range(16)]
        factor_rows, solved_rows = factor_tile(work, side, not last)
        factor_ref[mine, mine] = jnp.concatenate(factor_rows, axis=0)
        if last:
            gram_ref[4, mine, :] = jnp.concatenate(solved_rows, axis=0)
            break
        inverse = jnp.concatenate(solved_rows, axis=0)
        right = jnp.concatenate([gram_ref[w, mine, :] for w in range(p + 1, 5)], axis=1)
        solved = float_product(three_terms(inverse), three_terms(right), (1, 0))
        terms = three_terms(solved)
        for w in range(p + 1, 5):
            part = solved[:, 128 * (w - p - 1) : 128 * (w - p)]
            if w < 4:
                factor_ref[mine, 128 * w : 128 * w + 128] = part
            else:
                gram_ref[w, mine, :] = part
        for i in range(p + 1, 4):
            at = 128 * (i - p - 1)
            change = float_product([term[:, at : at + 128] for term in terms], [term[:, at:] for term in terms], (0, 0))
            for w in range(i, 5):
                gram_ref[w, 128 * i : 128 * i + 128, :] -= change[:, 128 * (w - i) : 128 * (w - i) + 128]
    diagonal_mask = lax.broadcasted_iota(jnp.int32, (128, 128), 0) == lax.broadcasted_iota(jnp.int32, (128, 128), 1)
    for p in range(4):
        tile = gram_ref[4, 128 * p : 128 * p + 128, :]
        proj_ref[:, 128 * p : 128 * p + 128] = jnp.sum(jnp.where(diagonal_mask, tile, 0.0), axis=0, keepdims=True)


def factorize(sums, smoothing):
    return pl.pallas_call(
        factor_kernel,
        out_shape=(
            jax.ShapeDtypeStruct((WIDTH, WIDTH), F32),
            jax.ShapeDtypeStruct((1, WIDTH), F32),
        ),
        scratch_shapes=[
            pltpu.VMEM((4, WIDTH, 128), F32),
            pltpu.VMEM((5, WIDTH, 128), F32),
        ],
        compiler_params=pltpu.CompilerParams(vmem_limit_bytes=40 * 1024 * 1024),
        name="factorize",
    )(sums, smoothing[None, :])


NEAR = ("zn", "yn", "core", "x")
FAR = ("zf", "zn", "yf", "yn")
FAR_GROUPS = [
    [((zf * 2 + (z ^ turn(zf))) * 4 + yf) * 2 + (y ^ turn(yf)) for zf in range(4) for yf in range(4)]
    for z in range(2)
    for y in range(2)
]


def exchange(rows, axes, parts, groups=None):
    split = rows.reshape(parts, -1, 128)
    return lax.all_to_all(split, axes, 0, 0, tiled=True, axis_index_groups=groups).reshape(-1, 128)


def per_device(covariates, intervals, offsets, responses, counts, smoothing):
    sums = local_sums(counts, covariates, intervals, offsets, responses)
    shares = sum_repeat(exchange(sums, NEAR, SHARES), SHARES, 16)
    shares = sum_repeat(exchange(shares, FAR, 16, FAR_GROUPS), 16, SHARES)
    factor, projected = factorize(exchange(shares, NEAR, SHARES), smoothing)
    return factor, projected[0]


def solution(mesh):
    fine = Mesh(mesh.devices.reshape(4, 2, 4, 2, 2, 4), ("zf", "zn", "yf", "yn", "core", "x"))
    spread = fine.axis_names
    return jax.shard_map(
        per_device,
        mesh=fine,
        in_specs=(P(None, spread), P(spread), P(spread), P(spread), P(spread), P()),
        out_specs=(P(), P()),
        check_vma=False,
    )
```

```python
import math

import jax
import jax.numpy as jnp
import numpy as np
from jax import lax
from jax.experimental import pallas as pl
from jax.experimental.pallas import tpu as pltpu
from jax.sharding import Mesh, PartitionSpec as P

P_COV = 64
N_BASIS = 8
WIDTH = P_COV * N_BASIS
CHUNK = 2048
UNROLL = 2
TOTAL_LIVE = 2097152
F32 = jnp.float32
BF16 = jnp.bfloat16
HIGHEST = lax.Precision.HIGHEST

ROW_SLABS = [(0, 0, 4), (0, 1, 1), (0, 2, 2), (0, 3, 3), (1, 2, 6), (1, 3, 3), (1, 4, 4), (1, 5, 5)]
ROW_SLABS += [(2, 4, 4), (2, 5, 5), (2, 6, 6), (2, 7, 7), (3, 6, 6), (3, 7, 7)]
HALF = len(ROW_SLABS) // 2
SHARES = 32
SHARE_ROWS = 16
SLAB_ROWS = SHARES * SHARE_ROWS
NT = (((1,), (1,)), ((), ()))
TN = (((0,), (0,)), ((), ()))


HI_SUMS = [(0, 7), (0, 6), (1, 7)]
LO_SUMS = [(0, 7), (0, 5), (1, 6), (2, 7)]
MID_ROWS = [8, 1, 6, 2, 3, 4, 5]
MID_PLACE = {0: 0, 7: 0, 1: 1, 6: 2, 2: 3, 3: 4, 4: 5, 5: 6}
END_HI_ROWS = [9, 10]
END_LO_ROWS = [9, 10, 11, 3, 4]


def basis_rows(j):
    return slice(j * P_COV, (j + 1) * P_COV)


def turn(far):
    return 1 - ((far + 1) // 2) % 2


def block_rows(i):
    exchanged = 4 * turn(lax.axis_index("zf")) + 2 * turn(lax.axis_index("yf"))
    return pl.ds(pl.multiple_of(jnp.bitwise_xor(jnp.int32(i), exchanged) * P_COV, P_COV), P_COV)


def slab_masks():
    row = lax.broadcasted_iota(jnp.int32, (P_COV, 128), 0)
    column = lax.broadcasted_iota(jnp.int32, (P_COV, 128), 1)
    return row, column % P_COV, column < P_COV


def gram_kernel(
    count_hbm, cov_hbm, int_hbm, off_hbm, resp_hbm, out_ref,
    count_ref, cov_ref, int_ref, off_ref, resp_ref, hi_even, hi_odd, lo_even, lo_odd, mid_ref, end_ref, mom_ref, row_sem, cov_sem,
):
    chunks = cov_hbm.shape[1] // CHUNK

    def columns(c):
        return pl.ds(pl.multiple_of(c * CHUNK, CHUNK), CHUNK)

    row_copies = [
        pltpu.make_async_copy(source, target, row_sem.at[i])
        for i, (source, target) in enumerate(
            [(count_hbm, count_ref), (int_hbm, int_ref), (off_hbm, off_ref), (resp_hbm, resp_ref)]
        )
    ]
    groups = chunks // UNROLL

    def cov_copy(i):
        part = pl.ds(pl.multiple_of(i * UNROLL * CHUNK, UNROLL * CHUNK), UNROLL * CHUNK)
        return pltpu.make_async_copy(cov_hbm.at[:, part], cov_ref.at[:, part], cov_sem.at[i])

    for copy in row_copies:
        copy.start()
    for i in range(groups):
        cov_copy(i).start()
    mid_ref[...] = jnp.zeros_like(mid_ref)
    end_ref[...] = jnp.zeros_like(end_ref)
    mom_ref[...] = jnp.zeros_like(mom_ref)
    for copy in row_copies:
        copy.wait()
    count = count_ref[0, 0]

    def build(c, hi_ref, lo_ref):
        part = columns(c)
        cov = cov_ref[:, part]
        interval = int_ref[:, part]
        within = off_ref[:, part]
        slot = lax.broadcasted_iota(jnp.int32, (1, CHUNK), 1) + c * CHUNK
        live = jnp.where(slot < count, 1.0, 0.0).astype(F32)
        square = within * within
        cube = square * within
        rest = 1.0 - within
        first = rest * rest * rest * (1.0 / 6.0) * live
        second = (3.0 * cube - 6.0 * square + 4.0) * (1.0 / 6.0) * live
        third = (-3.0 * cube + 3.0 * square + 3.0 * within + 1.0) * (1.0 / 6.0) * live
        fourth = cube * (1.0 / 6.0) * live
        weights, highs, lows = [], [], []
        for j in range(N_BASIS):
            value = jnp.where(interval == j, first, 0.0)
            value = jnp.where(interval + 1 == j, second, value)
            value = jnp.where(interval + 2 == j, third, value)
            value = jnp.where(interval + 3 == j, fourth, value)
            weights.append(value)
            design = cov * value
            highs.append(design.astype(BF16))
            lows.append((design - highs[j].astype(F32)).astype(BF16))
            hi_ref[basis_rows(j), :] = highs[j]
            lo_ref[basis_rows(j), :] = lows[j]
        for i, (j, k) in enumerate(HI_SUMS):
            hi_ref[basis_rows(N_BASIS + i), :] = highs[j] + highs[k]
        for i, (j, k) in enumerate(LO_SUMS):
            lo_ref[basis_rows(N_BASIS + i), :] = lows[j] + lows[k]
        cov_high = cov.astype(BF16)
        cov_low = (cov - cov_high.astype(F32)).astype(BF16)
        weighted = jnp.concatenate(weights, axis=0) * resp_ref[:, part]
        weighted_high = weighted.astype(BF16)
        weighted_low = (weighted - weighted_high.astype(F32)).astype(BF16)
        mom_ref[...] += lax.dot_general(
            jnp.concatenate([weighted_high, weighted_low], axis=0),
            jnp.concatenate([cov_high, cov_low], axis=0),
            NT,
            preferred_element_type=F32,
        )

    def multiply(hi_ref, lo_ref):
        def rows_of(ref, places):
            return [ref[basis_rows(place), :] for place in places]

        middle = jnp.concatenate(rows_of(hi_ref, MID_ROWS) + rows_of(lo_ref, MID_ROWS), axis=0)
        mid_ref[...] += lax.dot_general(middle, hi_ref[128:384, :], NT, preferred_element_type=F32)
        ends = jnp.concatenate(rows_of(hi_ref, END_HI_ROWS) + rows_of(lo_ref, END_LO_ROWS), axis=0)
        across = jnp.concatenate([hi_ref[0:128, :], hi_ref[384:512, :]], axis=0)
        end_ref[...] += lax.dot_general(ends, across, NT, preferred_element_type=F32)

    def group(i, _):
        cov_copy(i).wait()
        for c in range(UNROLL):
            hi_ref, lo_ref = (hi_odd, lo_odd) if c % 2 else (hi_even, lo_even)
            build(UNROLL * i + c, hi_ref, lo_ref)
            multiply(hi_ref, lo_ref)
        return 0

    def unused(i, _):
        cov_copy(i).wait()
        return 0

    used = pl.cdiv(count, UNROLL * CHUNK)
    lax.fori_loop(0, used, group, 0)
    lax.fori_loop(used, groups, unused, 0)

    row, column, left = slab_masks()
    tiles = {}

    def high_rows(j, w):
        if w in (1, 2):
            return mid_ref[basis_rows(MID_PLACE[j]), 128 * w - 128 : 128 * w]
        return end_ref[basis_rows(j % 6), 0:128] if w == 0 else end_ref[basis_rows(j - 6), 128:256]

    def low_rows(j, w):
        if w in (1, 2):
            return mid_ref[basis_rows(len(MID_ROWS) + MID_PLACE[j]), 128 * w - 128 : 128 * w]
        place = len(END_HI_ROWS) + (j if j < 5 else j - 5)
        return end_ref[basis_rows(place), 0:128] if w == 0 else end_ref[basis_rows(place), 128:256]

    def tile(t, w):
        turn_high = w == 0 and t in (1, 2)
        straight = [low_rows(j, w) if turn_high else low_rows(j, w) + high_rows(j, w) for j in (2 * t, 2 * t + 1)]
        turned = [low_rows(k, t) + high_rows(k, t) if turn_high else low_rows(k, t) for k in (2 * w, 2 * w + 1)]
        return jnp.concatenate(straight, axis=0) + jnp.concatenate(turned, axis=0).T

    def row_slab(entry):
        w, j_left, j_right = entry
        pieces = []
        for j in (j_left, j_right):
            t = j // 2
            if (t, w) not in tiles:
                tiles[t, w] = tile(t, w)
            pieces.append(tiles[t, w][(j % 2) * P_COV : (j % 2 + 1) * P_COV, :])
        return pieces[0] if j_left == j_right else jnp.where(left, pieces[0], pieces[1])

    small = [jnp.zeros((P_COV, 128), F32)]
    for i in range(HALF):
        upper, lower = row_slab(ROW_SLABS[i]), row_slab(ROW_SLABS[HALF + i])
        out_ref[block_rows(i), :] = jnp.where(row <= column, upper, lower)
        diagonal = jnp.sum(jnp.where(row == column, lower, 0.0), axis=0, keepdims=True)
        small.append(jnp.where(row == i, diagonal, small[-1]))
    mom = mom_ref[...]
    moment = mom[0:8, :] + mom[8:16, :] + pltpu.roll(mom[0:8, :], P_COV, 1)
    out_ref[block_rows(HALF), :] = jnp.concatenate([small[-1][0:8], moment, small[-1][16:]], axis=0)


def local_sums(count, covariates, intervals, offsets, responses):
    slots = covariates.shape[1]
    in_place = pl.BlockSpec(memory_space=pltpu.HBM)
    high = pltpu.VMEM((WIDTH + len(HI_SUMS) * P_COV, CHUNK), BF16)
    low = pltpu.VMEM((WIDTH + len(LO_SUMS) * P_COV, CHUNK), BF16)
    return pl.pallas_call(
        gram_kernel,
        in_specs=[in_place] * 5,
        out_shape=jax.ShapeDtypeStruct((SLAB_ROWS, 128), F32),
        scratch_shapes=[
            pltpu.SMEM((1, 1), jnp.int32),
            pltpu.VMEM((P_COV, slots), F32),
            pltpu.VMEM((1, slots), jnp.int32),
            pltpu.VMEM((1, slots), F32),
            pltpu.VMEM((1, slots), F32),
            high,
            high,
            low,
            low,
            pltpu.VMEM((2 * len(MID_ROWS) * P_COV, 256), F32),
            pltpu.VMEM(((len(END_HI_ROWS) + len(END_LO_ROWS)) * P_COV, 256), F32),
            pltpu.VMEM((16, 128), F32),
            pltpu.SemaphoreType.DMA((4,)),
            pltpu.SemaphoreType.DMA((slots // (UNROLL * CHUNK),)),
        ],
        compiler_params=pltpu.CompilerParams(vmem_limit_bytes=62 * 1024 * 1024),
        name="local_sums",
    )(count[None, :], covariates, intervals[None, :], offsets[None, :], responses[None, :])


def sum_repeat_kernel(parts, copies, in_ref, out_ref):
    rows = in_ref.shape[0] // parts
    total = in_ref[0:rows, :]
    for i in range(1, parts):
        total = total + in_ref[i * rows : (i + 1) * rows, :]
    for i in range(copies):
        out_ref[i * rows : (i + 1) * rows, :] = total


def sum_repeat(received, parts, copies):
    rows = received.shape[0] // parts
    return pl.pallas_call(
        lambda a, b: sum_repeat_kernel(parts, copies, a, b),
        out_shape=jax.ShapeDtypeStruct((copies * rows, 128), F32),
        compiler_params=pltpu.CompilerParams(vmem_limit_bytes=4 * 1024 * 1024),
        name="sum_repeat",
    )(received)


def lane_spread(tile, lane):
    return jnp.take_along_axis(tile, jnp.full(tile.shape, lane, jnp.int32), axis=1)


def row_spread(tile, row):
    return jnp.broadcast_to(tile[row : row + 1, :], tile.shape)


def three_terms(value):
    high = value.astype(BF16)
    rest = value - high.astype(F32)
    middle = rest.astype(BF16)
    return high, middle, (rest - middle.astype(F32)).astype(BF16)


TERM_PAIRS = [(0, 0), (0, 1), (1, 0), (1, 1), (0, 2), (2, 0)]


def float_product(left_terms, right_terms, contract):
    left_axis, right_axis = contract
    return lax.dot_general(
        jnp.concatenate([left_terms[i] for i, _ in TERM_PAIRS], axis=left_axis),
        jnp.concatenate([right_terms[i] for _, i in TERM_PAIRS], axis=right_axis),
        (((left_axis,), (right_axis,)), ((), ())),
        preferred_element_type=F32,
    )


def factor_tile(work, side, side_is_identity):
    blocks = len(work)
    lanes = lax.broadcasted_iota(jnp.int32, (8, 128), 1)
    subs = lax.broadcasted_iota(jnp.int32, (8, 128), 0)
    factor_rows, solved_rows = [], []
    for k in range(blocks):
        if k == 0:
            columns = [lane_spread(work[0], t) for t in range(8)]
        if k + 1 < blocks:
            ahead = [lane_spread(work[k + 1], 8 * k + 8 + t) for t in range(8)]
        entry = {(s, t): row_spread(columns[t], s) for t in range(8) for s in range(t, 8)}
        rows = [row_spread(work[k], t) for t in range(8)]
        siderows = [row_spread(side[k], t) for t in range(8)]
        pivot = entry[0, 0]
        pivots, reciprocals, scale = [], [], {}
        for t in range(8):
            reciprocal = 1.0 / pivot
            pivots.append(pivot)
            reciprocals.append(reciprocal)
            if t + 1 < 8:
                pivot = entry[t + 1, t + 1] - (entry[t + 1, t] * entry[t + 1, t]) * reciprocal
            for s in range(t + 1, 8):
                scale[s, t] = entry[s, t] * reciprocal
            for s in range(t + 1, 8):
                for u in range(t + 1, s + 1):
                    if (s, u) != (t + 1, t + 1):
                        entry[s, u] = entry[s, u] - scale[s, t] * entry[u, t]
                rows[s] = rows[s] - scale[s, t] * rows[t]
                siderows[s] = siderows[s] - scale[s, t] * siderows[t]
        near = k + 3 if k % 2 else k + 4
        for b in range(k + 1, min(near, blocks)):
            c = [lane_spread(work[b], 8 * k + t) for t in range(8)]
            for t in range(8):
                for s in range(t + 1, 8):
                    c[s] = c[s] - scale[s, t] * c[t]
                weight = c[t] * reciprocals[t]
                work[b] = work[b] - weight * rows[t]
                side[b] = side[b] - weight * siderows[t]
                if b == k + 1:
                    ahead = [ahead[u] - weight * row_spread(c[t], u) for u in range(8)]
        if k + 1 < blocks:
            columns = ahead
        out, sideout = jnp.zeros((8, 128), F32), jnp.zeros((8, 128), F32)
        for t in range(8):
            root = lax.rsqrt(pivots[t])
            out = jnp.where(subs == t, rows[t] * root, out)
            sideout = jnp.where(subs == t, siderows[t] * root, sideout)
        factor_rows.append(jnp.where(lanes >= subs + 8 * k, out, 0.0))
        solved_rows.append(jnp.where(lanes <= subs + 8 * k, sideout, 0.0) if side_is_identity else sideout)
        if k % 2 and near < blocks:
            upper = jnp.concatenate(factor_rows[k - 1 :], axis=0)
            both = jnp.concatenate([upper, jnp.concatenate(solved_rows[k - 1 :], axis=0)], axis=1)
            change = float_product(three_terms(upper), three_terms(both), (0, 0))
            for b in range(near, blocks):
                work[b] = work[b] - change[8 * b : 8 * b + 8, :128]
                side[b] = side[b] - change[8 * b : 8 * b + 8, 128:]
    return factor_rows, solved_rows


def factor_kernel(sums_ref, smooth_ref, factor_ref, proj_ref, half_ref, gram_ref):
    row, column, left = slab_masks()
    second = np.zeros((N_BASIS - 2, N_BASIS))
    for i in range(N_BASIS - 2):
        second[i, i : i + 3] = (1.0, -2.0, 1.0)
    penalty = second.T @ second
    smooth = jnp.where(row == column, jnp.concatenate([smooth_ref[...], smooth_ref[...]], axis=1), 0.0)
    small = sums_ref[block_rows(HALF), :]
    diagonals = small[0:8]
    diagonals = (diagonals, pltpu.roll(diagonals, P_COV, 1))
    packed, turned = {}, {}
    for i in range(0, HALF, 2):
        both = jnp.concatenate([sums_ref[block_rows(i), :], sums_ref[block_rows(i + 1), :]], axis=0)
        top, bottom = both.T[:P_COV], both.T[P_COV:]
        top_moved, bottom_moved = pltpu.roll(top, P_COV, 1), pltpu.roll(bottom, P_COV, 1)
        packed[i], packed[i + 1] = both[:P_COV], both[P_COV:]
        turned[i, 0] = jnp.where(left, top, bottom_moved)
        turned[i, 1] = jnp.where(left, bottom, top_moved)
        turned[i + 1, 0] = jnp.where(left, top_moved, bottom)
        turned[i + 1, 1] = jnp.where(left, bottom_moved, top)
    place, slabs = {}, {}
    for number, (w, j_left, j_right) in enumerate(ROW_SLABS):
        place[j_left, 2 * w] = number
        if j_right >= 2 * w + 1:
            place[j_right, 2 * w + 1] = number

    def slab(number, swap):
        if (number, swap) not in slabs:
            i = number % HALF
            straight = pltpu.roll(packed[i], P_COV, 1) if swap else packed[i]
            if number < HALF:
                value = jnp.where(row <= column, straight, turned[i, swap])
            else:
                diagonal = jnp.broadcast_to(diagonals[swap][i : i + 1, :], (P_COV, 128))
                value = jnp.where(row > column, straight, turned[i, swap])
                value = jnp.where(row == column, diagonal, value)
            w, j_left, j_right = ROW_SLABS[number]
            factors = (float(penalty[j_left, 2 * w]), float(penalty[j_right, 2 * w + 1]))
            scale = jnp.where(left, factors[swap], factors[1 - swap])
            slabs[number, swap] = value * (1.0 / TOTAL_LIVE) + smooth * scale
        return slabs[number, swap]

    def in_half(j, k, half):
        pair = (max(j, k), min(j, k))
        return slab(place[pair], int(pair[1] % 2 != half)) if pair in place else None

    nothing = jnp.zeros((P_COV, 128), F32)
    for j in range(N_BASIS):
        for w in range(4):
            first, second = in_half(j, 2 * w, 0), in_half(j, 2 * w + 1, 1)
            first, second = (nothing if first is None else first), (nothing if second is None else second)
            half_ref[w, pl.ds(j, P_COV, N_BASIS), :] = first if first is second else jnp.where(left, first, second)
    for w in range(4):
        for i in range(4):
            turned = half_ref[w, 128 * i : 128 * i + 128, :].T
            above = 16 * (i + 1)
            for k in (2 * w, 2 * w + 1):
                gram_ref[i, pl.ds(k, above, N_BASIS), :] = turned[(k - 2 * w) * P_COV : (k - 2 * w) * P_COV + above, :]
    moment = small[8:16, 0:P_COV].T * (1.0 / math.sqrt(TOTAL_LIVE))
    for j in range(N_BASIS):
        gram_ref[4, pl.ds(j, P_COV, N_BASIS), :] = jnp.broadcast_to(moment[:, j : j + 1], (P_COV, 128))

    factor_ref[...] = jnp.zeros_like(factor_ref)
    lanes = lax.broadcasted_iota(jnp.int32, (8, 128), 1)
    subs = lax.broadcasted_iota(jnp.int32, (8, 128), 0)

    for p in range(4):
        mine = slice(128 * p, 128 * p + 128)
        work = [gram_ref[p, 128 * p + 8 * b : 128 * p + 8 * b + 8, :] for b in range(16)]
        last = p == 3
        if last:
            side = [gram_ref[4, 128 * p + 8 * b : 128 * p + 8 * b + 8, :] for b in range(16)]
        else:
            side = [jnp.where(lanes == subs + 8 * b, 1.0, 0.0).astype(F32) for b in range(16)]
        factor_rows, solved_rows = factor_tile(work, side, not last)
        factor_ref[mine, mine] = jnp.concatenate(factor_rows, axis=0)
        if last:
            gram_ref[4, mine, :] = jnp.concatenate(solved_rows, axis=0)
            break
        inverse = jnp.concatenate(solved_rows, axis=0)
        right = jnp.concatenate([gram_ref[w, mine, :] for w in range(p + 1, 5)], axis=1)
        solved = float_product(three_terms(inverse), three_terms(right), (1, 0))
        terms = three_terms(solved)
        for w in range(p + 1, 5):
            part = solved[:, 128 * (w - p - 1) : 128 * (w - p)]
            if w < 4:
                factor_ref[mine, 128 * w : 128 * w + 128] = part
            else:
                gram_ref[w, mine, :] = part
        for i in range(p + 1, 4):
            at = 128 * (i - p - 1)
            change = float_product([term[:, at : at + 128] for term in terms], [term[:, at:] for term in terms], (0, 0))
            for w in range(i, 5):
                gram_ref[w, 128 * i : 128 * i + 128, :] -= change[:, 128 * (w - i) : 128 * (w - i) + 128]
    diagonal_mask = lax.broadcasted_iota(jnp.int32, (128, 128), 0) == lax.broadcasted_iota(jnp.int32, (128, 128), 1)
    for p in range(4):
        tile = gram_ref[4, 128 * p : 128 * p + 128, :]
        proj_ref[:, 128 * p : 128 * p + 128] = jnp.sum(jnp.where(diagonal_mask, tile, 0.0), axis=0, keepdims=True)


def factorize(sums, smoothing):
    return pl.pallas_call(
        factor_kernel,
        out_shape=(
            jax.ShapeDtypeStruct((WIDTH, WIDTH), F32),
            jax.ShapeDtypeStruct((1, WIDTH), F32),
        ),
        scratch_shapes=[
            pltpu.VMEM((4, WIDTH, 128), F32),
            pltpu.VMEM((5, WIDTH, 128), F32),
        ],
        compiler_params=pltpu.CompilerParams(vmem_limit_bytes=40 * 1024 * 1024),
        name="factorize",
    )(sums, smoothing[None, :])


NEAR = ("zn", "yn", "core", "x")
FAR = ("zf", "zn", "yf", "yn")
FAR_GROUPS = [
    [((zf * 2 + (z ^ turn(zf))) * 4 + yf) * 2 + (y ^ turn(yf)) for zf in range(4) for yf in range(4)]
    for z in range(2)
    for y in range(2)
]


def exchange(rows, axes, parts, groups=None):
    split = rows.reshape(parts, -1, 128)
    return lax.all_to_all(split, axes, 0, 0, tiled=True, axis_index_groups=groups).reshape(-1, 128)


def per_device(covariates, intervals, offsets, responses, counts, smoothing):
    sums = local_sums(counts, covariates, intervals, offsets, responses)
    shares = sum_repeat(exchange(sums, NEAR, SHARES), SHARES, 16)
    shares = sum_repeat(exchange(shares, FAR, 16, FAR_GROUPS), 16, SHARES)
    factor, projected = factorize(exchange(shares, NEAR, SHARES), smoothing)
    return factor, projected[0]


def solution(mesh):
    fine = Mesh(mesh.devices.reshape(4, 2, 4, 2, 2, 4), ("zf", "zn", "yf", "yn", "core", "x"))
    spread = fine.axis_names
    return jax.shard_map(
        per_device,
        mesh=fine,
        in_specs=(P(None, spread), P(spread), P(spread), P(spread), P(spread), P()),
        out_specs=(P(), P()),
        check_vma=False,
    )
```

```python
import math

import jax
import jax.numpy as jnp
import numpy as np
from jax import lax
from jax.experimental import pallas as pl
from jax.experimental.pallas import tpu as pltpu
from jax.sharding import Mesh, PartitionSpec as P

P_COV = 64
N_BASIS = 8
WIDTH = P_COV * N_BASIS
CHUNK = 2048
UNROLL = 2
TOTAL_LIVE = 2097152
F32 = jnp.float32
BF16 = jnp.bfloat16
HIGHEST = lax.Precision.HIGHEST

ROW_SLABS = [(0, 0, 4), (0, 1, 1), (0, 2, 2), (0, 3, 3), (1, 2, 6), (1, 3, 3), (1, 4, 4), (1, 5, 5)]
ROW_SLABS += [(2, 4, 4), (2, 5, 5), (2, 6, 6), (2, 7, 7), (3, 6, 6), (3, 7, 7)]
HALF = len(ROW_SLABS) // 2
SHARES = 32
SHARE_ROWS = 16
SLAB_ROWS = SHARES * SHARE_ROWS
NT = (((1,), (1,)), ((), ()))
TN = (((0,), (0,)), ((), ()))


HI_SUMS = [(0, 7), (0, 6), (1, 7)]
LO_SUMS = [(0, 7), (0, 5), (1, 6), (2, 7)]
MID_ROWS = [8, 1, 6, 2, 3, 4, 5]
MID_PLACE = {0: 0, 7: 0, 1: 1, 6: 2, 2: 3, 3: 4, 4: 5, 5: 6}
END_HI_ROWS = [9, 10]
END_LO_ROWS = [9, 10, 11, 3, 4]


def basis_rows(j):
    return slice(j * P_COV, (j + 1) * P_COV)


def turn(far):
    return 1 - ((far + 1) // 2) % 2


def block_rows(i):
    exchanged = 4 * turn(lax.axis_index("zf")) + 2 * turn(lax.axis_index("yf"))
    return pl.ds(pl.multiple_of(jnp.bitwise_xor(jnp.int32(i), exchanged) * P_COV, P_COV), P_COV)


def slab_masks():
    row = lax.broadcasted_iota(jnp.int32, (P_COV, 128), 0)
    column = lax.broadcasted_iota(jnp.int32, (P_COV, 128), 1)
    return row, column % P_COV, column < P_COV


def gram_kernel(
    count_hbm, cov_hbm, int_hbm, off_hbm, resp_hbm, out_ref,
    count_ref, cov_ref, int_ref, off_ref, resp_ref, hi_even, hi_odd, lo_even, lo_odd, mid_ref, end_ref, mom_ref, row_sem, cov_sem,
):
    chunks = cov_hbm.shape[1] // CHUNK

    def columns(c):
        return pl.ds(pl.multiple_of(c * CHUNK, CHUNK), CHUNK)

    row_copies = [
        pltpu.make_async_copy(source, target, row_sem.at[i])
        for i, (source, target) in enumerate(
            [(count_hbm, count_ref), (int_hbm, int_ref), (off_hbm, off_ref), (resp_hbm, resp_ref)]
        )
    ]
    groups = chunks // UNROLL

    def cov_copy(i):
        part = pl.ds(pl.multiple_of(i * UNROLL * CHUNK, UNROLL * CHUNK), UNROLL * CHUNK)
        return pltpu.make_async_copy(cov_hbm.at[:, part], cov_ref.at[:, part], cov_sem.at[i])

    for copy in row_copies:
        copy.start()
    for i in range(groups):
        cov_copy(i).start()
    mid_ref[...] = jnp.zeros_like(mid_ref)
    end_ref[...] = jnp.zeros_like(end_ref)
    mom_ref[...] = jnp.zeros_like(mom_ref)
    for copy in row_copies:
        copy.wait()
    count = count_ref[0, 0]

    def build(c, hi_ref, lo_ref):
        part = columns(c)
        cov = cov_ref[:, part]
        interval = int_ref[:, part]
        within = off_ref[:, part]
        slot = lax.broadcasted_iota(jnp.int32, (1, CHUNK), 1) + c * CHUNK
        live = jnp.where(slot < count, 1.0, 0.0).astype(F32)
        square = within * within
        cube = square * within
        rest = 1.0 - within
        first = rest * rest * rest * (1.0 / 6.0) * live
        second = (3.0 * cube - 6.0 * square + 4.0) * (1.0 / 6.0) * live
        third = (-3.0 * cube + 3.0 * square + 3.0 * within + 1.0) * (1.0 / 6.0) * live
        fourth = cube * (1.0 / 6.0) * live
        weights, highs, lows = [], [], []
        for j in range(N_BASIS):
            value = jnp.where(interval == j, first, 0.0)
            value = jnp.where(interval + 1 == j, second, value)
            value = jnp.where(interval + 2 == j, third, value)
            value = jnp.where(interval + 3 == j, fourth, value)
            weights.append(value)
            design = cov * value
            highs.append(design.astype(BF16))
            lows.append((design - highs[j].astype(F32)).astype(BF16))
            hi_ref[basis_rows(j), :] = highs[j]
            lo_ref[basis_rows(j), :] = lows[j]
        for i, (j, k) in enumerate(HI_SUMS):
            hi_ref[basis_rows(N_BASIS + i), :] = highs[j] + highs[k]
        for i, (j, k) in enumerate(LO_SUMS):
            lo_ref[basis_rows(N_BASIS + i), :] = lows[j] + lows[k]
        cov_high = cov.astype(BF16)
        cov_low = (cov - cov_high.astype(F32)).astype(BF16)
        weighted = jnp.concatenate(weights, axis=0) * resp_ref[:, part]
        weighted_high = weighted.astype(BF16)
        weighted_low = (weighted - weighted_high.astype(F32)).astype(BF16)
        mom_ref[...] += lax.dot_general(
            jnp.concatenate([weighted_high, weighted_low], axis=0),
            jnp.concatenate([cov_high, cov_low], axis=0),
            NT,
            preferred_element_type=F32,
        )

    def multiply(hi_ref, lo_ref):
        def rows_of(ref, places):
            return [ref[basis_rows(place), :] for place in places]

        middle = jnp.concatenate(rows_of(hi_ref, MID_ROWS) + rows_of(lo_ref, MID_ROWS), axis=0)
        mid_ref[...] += lax.dot_general(middle, hi_ref[128:384, :], NT, preferred_element_type=F32)
        ends = jnp.concatenate(rows_of(hi_ref, END_HI_ROWS) + rows_of(lo_ref, END_LO_ROWS), axis=0)
        across = jnp.concatenate([hi_ref[0:128, :], hi_ref[384:512, :]], axis=0)
        end_ref[...] += lax.dot_general(ends, across, NT, preferred_element_type=F32)

    def group(i, _):
        cov_copy(i).wait()
        for c in range(UNROLL):
            hi_ref, lo_ref = (hi_odd, lo_odd) if c % 2 else (hi_even, lo_even)
            build(UNROLL * i + c, hi_ref, lo_ref)
            multiply(hi_ref, lo_ref)
        return 0

    def unused(i, _):
        cov_copy(i).wait()
        return 0

    used = pl.cdiv(count, UNROLL * CHUNK)
    lax.fori_loop(0, used, group, 0)
    lax.fori_loop(used, groups, unused, 0)

    row, column, left = slab_masks()
    tiles = {}

    def high_rows(j, w):
        if w in (1, 2):
            return mid_ref[basis_rows(MID_PLACE[j]), 128 * w - 128 : 128 * w]
        return end_ref[basis_rows(j % 6), 0:128] if w == 0 else end_ref[basis_rows(j - 6), 128:256]

    def low_rows(j, w):
        if w in (1, 2):
            return mid_ref[basis_rows(len(MID_ROWS) + MID_PLACE[j]), 128 * w - 128 : 128 * w]
        place = len(END_HI_ROWS) + (j if j < 5 else j - 5)
        return end_ref[basis_rows(place), 0:128] if w == 0 else end_ref[basis_rows(place), 128:256]

    def tile(t, w):
        turn_high = w == 0 and t in (1, 2)
        straight = [low_rows(j, w) if turn_high else low_rows(j, w) + high_rows(j, w) for j in (2 * t, 2 * t + 1)]
        turned = [low_rows(k, t) + high_rows(k, t) if turn_high else low_rows(k, t) for k in (2 * w, 2 * w + 1)]
        return jnp.concatenate(straight, axis=0) + jnp.concatenate(turned, axis=0).T

    def row_slab(entry):
        w, j_left, j_right = entry
        pieces = []
        for j in (j_left, j_right):
            t = j // 2
            if (t, w) not in tiles:
                tiles[t, w] = tile(t, w)
            pieces.append(tiles[t, w][(j % 2) * P_COV : (j % 2 + 1) * P_COV, :])
        return pieces[0] if j_left == j_right else jnp.where(left, pieces[0], pieces[1])

    small = [jnp.zeros((P_COV, 128), F32)]
    for i in range(HALF):
        upper, lower = row_slab(ROW_SLABS[i]), row_slab(ROW_SLABS[HALF + i])
        out_ref[block_rows(i), :] = jnp.where(row <= column, upper, lower)
        diagonal = jnp.sum(jnp.where(row == column, lower, 0.0), axis=0, keepdims=True)
        small.append(jnp.where(row == i, diagonal, small[-1]))
    mom = mom_ref[...]
    moment = mom[0:8, :] + mom[8:16, :] + pltpu.roll(mom[0:8, :], P_COV, 1)
    out_ref[block_rows(HALF), :] = jnp.concatenate([small[-1][0:8], moment, small[-1][16:]], axis=0)


def local_sums(count, covariates, intervals, offsets, responses):
    slots = covariates.shape[1]
    in_place = pl.BlockSpec(memory_space=pltpu.HBM)
    high = pltpu.VMEM((WIDTH + len(HI_SUMS) * P_COV, CHUNK), BF16)
    low = pltpu.VMEM((WIDTH + len(LO_SUMS) * P_COV, CHUNK), BF16)
    return pl.pallas_call(
        gram_kernel,
        in_specs=[in_place] * 5,
        out_shape=jax.ShapeDtypeStruct((SLAB_ROWS, 128), F32),
        scratch_shapes=[
            pltpu.SMEM((1, 1), jnp.int32),
            pltpu.VMEM((P_COV, slots), F32),
            pltpu.VMEM((1, slots), jnp.int32),
            pltpu.VMEM((1, slots), F32),
            pltpu.VMEM((1, slots), F32),
            high,
            high,
            low,
            low,
            pltpu.VMEM((2 * len(MID_ROWS) * P_COV, 256), F32),
            pltpu.VMEM(((len(END_HI_ROWS) + len(END_LO_ROWS)) * P_COV, 256), F32),
            pltpu.VMEM((16, 128), F32),
            pltpu.SemaphoreType.DMA((4,)),
            pltpu.SemaphoreType.DMA((slots // (UNROLL * CHUNK),)),
        ],
        compiler_params=pltpu.CompilerParams(vmem_limit_bytes=62 * 1024 * 1024),
        name="local_sums",
    )(count[None, :], covariates, intervals[None, :], offsets[None, :], responses[None, :])


def sum_repeat_kernel(parts, copies, in_ref, out_ref):
    rows = in_ref.shape[0] // parts
    total = in_ref[0:rows, :]
    for i in range(1, parts):
        total = total + in_ref[i * rows : (i + 1) * rows, :]
    for i in range(copies):
        out_ref[i * rows : (i + 1) * rows, :] = total


def sum_repeat(received, parts, copies):
    rows = received.shape[0] // parts
    return pl.pallas_call(
        lambda a, b: sum_repeat_kernel(parts, copies, a, b),
        out_shape=jax.ShapeDtypeStruct((copies * rows, 128), F32),
        compiler_params=pltpu.CompilerParams(vmem_limit_bytes=4 * 1024 * 1024),
        name="sum_repeat",
    )(received)


def lane_spread(tile, lane):
    return jnp.take_along_axis(tile, jnp.full(tile.shape, lane, jnp.int32), axis=1)


def row_spread(tile, row):
    return jnp.broadcast_to(tile[row : row + 1, :], tile.shape)


def three_terms(value):
    high = value.astype(BF16)
    rest = value - high.astype(F32)
    middle = rest.astype(BF16)
    return high, middle, (rest - middle.astype(F32)).astype(BF16)


TERM_PAIRS = [(0, 0), (0, 1), (1, 0), (1, 1), (0, 2), (2, 0)]


def float_product(left_terms, right_terms, contract):
    left_axis, right_axis = contract
    return lax.dot_general(
        jnp.concatenate([left_terms[i] for i, _ in TERM_PAIRS], axis=left_axis),
        jnp.concatenate([right_terms[i] for _, i in TERM_PAIRS], axis=right_axis),
        (((left_axis,), (right_axis,)), ((), ())),
        preferred_element_type=F32,
    )


def factor_tile(work, side, side_is_identity):
    blocks = len(work)
    lanes = lax.broadcasted_iota(jnp.int32, (8, 128), 1)
    subs = lax.broadcasted_iota(jnp.int32, (8, 128), 0)
    factor_rows, solved_rows = [], []
    for k in range(blocks):
        if k == 0:
            columns = [lane_spread(work[0], t) for t in range(8)]
        if k + 1 < blocks:
            ahead = [lane_spread(work[k + 1], 8 * k + 8 + t) for t in range(8)]
        entry = {(s, t): row_spread(columns[t], s) for t in range(8) for s in range(t, 8)}
        rows = [row_spread(work[k], t) for t in range(8)]
        siderows = [row_spread(side[k], t) for t in range(8)]
        pivot = entry[0, 0]
        pivots, reciprocals, scale = [], [], {}
        for t in range(8):
            reciprocal = 1.0 / pivot
            pivots.append(pivot)
            reciprocals.append(reciprocal)
            if t + 1 < 8:
                pivot = entry[t + 1, t + 1] - (entry[t + 1, t] * entry[t + 1, t]) * reciprocal
            for s in range(t + 1, 8):
                scale[s, t] = entry[s, t] * reciprocal
            for s in range(t + 1, 8):
                for u in range(t + 1, s + 1):
                    if (s, u) != (t + 1, t + 1):
                        entry[s, u] = entry[s, u] - scale[s, t] * entry[u, t]
                rows[s] = rows[s] - scale[s, t] * rows[t]
                siderows[s] = siderows[s] - scale[s, t] * siderows[t]
        near = k + 3 if k % 2 else k + 4
        for b in range(k + 1, min(near, blocks)):
            c = [lane_spread(work[b], 8 * k + t) for t in range(8)]
            for t in range(8):
                for s in range(t + 1, 8):
                    c[s] = c[s] - scale[s, t] * c[t]
                weight = c[t] * reciprocals[t]
                work[b] = work[b] - weight * rows[t]
                side[b] = side[b] - weight * siderows[t]
                if b == k + 1:
                    ahead = [ahead[u] - weight * row_spread(c[t], u) for u in range(8)]
        if k + 1 < blocks:
            columns = ahead
        out, sideout = jnp.zeros((8, 128), F32), jnp.zeros((8, 128), F32)
        for t in range(8):
            root = lax.rsqrt(pivots[t])
            out = jnp.where(subs == t, rows[t] * root, out)
            sideout = jnp.where(subs == t, siderows[t] * root, sideout)
        factor_rows.append(jnp.where(lanes >= subs + 8 * k, out, 0.0))
        solved_rows.append(jnp.where(lanes <= subs + 8 * k, sideout, 0.0) if side_is_identity else sideout)
        if k % 2 and near < blocks:
            upper = jnp.concatenate(factor_rows[k - 1 :], axis=0)
            both = jnp.concatenate([upper, jnp.concatenate(solved_rows[k - 1 :], axis=0)], axis=1)
            change = float_product(three_terms(upper), three_terms(both), (0, 0))
            for b in range(near, blocks):
                work[b] = work[b] - change[8 * b : 8 * b + 8, :128]
                side[b] = side[b] - change[8 * b : 8 * b + 8, 128:]
    return factor_rows, solved_rows


def factor_kernel(sums_ref, smooth_ref, factor_ref, proj_ref, half_ref, gram_ref):
    row, column, left = slab_masks()
    second = np.zeros((N_BASIS - 2, N_BASIS))
    for i in range(N_BASIS - 2):
        second[i, i : i + 3] = (1.0, -2.0, 1.0)
    penalty = second.T @ second
    smooth = jnp.where(row == column, jnp.concatenate([smooth_ref[...], smooth_ref[...]], axis=1), 0.0)
    small = sums_ref[block_rows(HALF), :]
    diagonals = small[0:8]
    diagonals = (diagonals, pltpu.roll(diagonals, P_COV, 1))
    packed, turned = {}, {}
    for i in range(0, HALF, 2):
        both = jnp.concatenate([sums_ref[block_rows(i), :], sums_ref[block_rows(i + 1), :]], axis=0)
        top, bottom = both.T[:P_COV], both.T[P_COV:]
        top_moved, bottom_moved = pltpu.roll(top, P_COV, 1), pltpu.roll(bottom, P_COV, 1)
        packed[i], packed[i + 1] = both[:P_COV], both[P_COV:]
        turned[i, 0] = jnp.where(left, top, bottom_moved)
        turned[i, 1] = jnp.where(left, bottom, top_moved)
        turned[i + 1, 0] = jnp.where(left, top_moved, bottom)
        turned[i + 1, 1] = jnp.where(left, bottom_moved, top)
    place, slabs = {}, {}
    for number, (w, j_left, j_right) in enumerate(ROW_SLABS):
        place[j_left, 2 * w] = number
        if j_right >= 2 * w + 1:
            place[j_right, 2 * w + 1] = number

    def slab(number, swap):
        if (number, swap) not in slabs:
            i = number % HALF
            straight = pltpu.roll(packed[i], P_COV, 1) if swap else packed[i]
            if number < HALF:
                value = jnp.where(row <= column, straight, turned[i, swap])
            else:
                diagonal = jnp.broadcast_to(diagonals[swap][i : i + 1, :], (P_COV, 128))
                value = jnp.where(row > column, straight, turned[i, swap])
                value = jnp.where(row == column, diagonal, value)
            w, j_left, j_right = ROW_SLABS[number]
            factors = (float(penalty[j_left, 2 * w]), float(penalty[j_right, 2 * w + 1]))
            scale = jnp.where(left, factors[swap], factors[1 - swap])
            slabs[number, swap] = value * (1.0 / TOTAL_LIVE) + smooth * scale
        return slabs[number, swap]

    def in_half(j, k, half):
        pair = (max(j, k), min(j, k))
        return slab(place[pair], int(pair[1] % 2 != half)) if pair in place else None

    nothing = jnp.zeros((P_COV, 128), F32)
    for j in range(N_BASIS):
        for w in range(4):
            first, second = in_half(j, 2 * w, 0), in_half(j, 2 * w + 1, 1)
            first, second = (nothing if first is None else first), (nothing if second is None else second)
            half_ref[w, pl.ds(j, P_COV, N_BASIS), :] = first if first is second else jnp.where(left, first, second)
    for w in range(4):
        for i in range(4):
            turned = half_ref[w, 128 * i : 128 * i + 128, :].T
            above = 16 * (i + 1)
            for k in (2 * w, 2 * w + 1):
                gram_ref[i, pl.ds(k, above, N_BASIS), :] = turned[(k - 2 * w) * P_COV : (k - 2 * w) * P_COV + above, :]
    moment = small[8:16, 0:P_COV].T * (1.0 / math.sqrt(TOTAL_LIVE))
    for j in range(N_BASIS):
        gram_ref[4, pl.ds(j, P_COV, N_BASIS), :] = jnp.broadcast_to(moment[:, j : j + 1], (P_COV, 128))

    factor_ref[...] = jnp.zeros_like(factor_ref)
    lanes = lax.broadcasted_iota(jnp.int32, (8, 128), 1)
    subs = lax.broadcasted_iota(jnp.int32, (8, 128), 0)

    for p in range(4):
        mine = slice(128 * p, 128 * p + 128)
        work = [gram_ref[p, 128 * p + 8 * b : 128 * p + 8 * b + 8, :] for b in range(16)]
        last = p == 3
        if last:
            side = [gram_ref[4, 128 * p + 8 * b : 128 * p + 8 * b + 8, :] for b in range(16)]
        else:
            side = [jnp.where(lanes == subs + 8 * b, 1.0, 0.0).astype(F32) for b in range(16)]
        factor_rows, solved_rows = factor_tile(work, side, not last)
        factor_ref[mine, mine] = jnp.concatenate(factor_rows, axis=0)
        if last:
            gram_ref[4, mine, :] = jnp.concatenate(solved_rows, axis=0)
            break
        inverse = jnp.concatenate(solved_rows, axis=0)
        right = jnp.concatenate([gram_ref[w, mine, :] for w in range(p + 1, 5)], axis=1)
        solved = float_product(three_terms(inverse), three_terms(right), (1, 0))
        terms = three_terms(solved)
        for w in range(p + 1, 5):
            part = solved[:, 128 * (w - p - 1) : 128 * (w - p)]
            if w < 4:
                factor_ref[mine, 128 * w : 128 * w + 128] = part
            else:
                gram_ref[w, mine, :] = part
        for i in range(p + 1, 4):
            at = 128 * (i - p - 1)
            change = float_product([term[:, at : at + 128] for term in terms], [term[:, at:] for term in terms], (0, 0))
            for w in range(i, 5):
                gram_ref[w, 128 * i : 128 * i + 128, :] -= change[:, 128 * (w - i) : 128 * (w - i) + 128]
    diagonal_mask = lax.broadcasted_iota(jnp.int32, (128, 128), 0) == lax.broadcasted_iota(jnp.int32, (128, 128), 1)
    for p in range(4):
        tile = gram_ref[4, 128 * p : 128 * p + 128, :]
        proj_ref[:, 128 * p : 128 * p + 128] = jnp.sum(jnp.where(diagonal_mask, tile, 0.0), axis=0, keepdims=True)


def factorize(sums, smoothing):
    return pl.pallas_call(
        factor_kernel,
        out_shape=(
            jax.ShapeDtypeStruct((WIDTH, WIDTH), F32),
            jax.ShapeDtypeStruct((1, WIDTH), F32),
        ),
        scratch_shapes=[
            pltpu.VMEM((4, WIDTH, 128), F32),
            pltpu.VMEM((5, WIDTH, 128), F32),
        ],
        compiler_params=pltpu.CompilerParams(vmem_limit_bytes=40 * 1024 * 1024),
        name="factorize",
    )(sums, smoothing[None, :])


NEAR = ("zn", "yn", "core", "x")
FAR = ("zf", "zn", "yf", "yn")
FAR_ORDER = [divmod(9 * i % 16, 4) for i in range(16)]
FAR_GROUPS = [
    [((zf * 2 + (z ^ turn(zf))) * 4 + yf) * 2 + (y ^ turn(yf)) for zf, yf in FAR_ORDER]
    for z in range(2)
    for y in range(2)
]


def exchange(rows, axes, parts, groups=None):
    split = rows.reshape(parts, -1, 128)
    return lax.all_to_all(split, axes, 0, 0, tiled=True, axis_index_groups=groups).reshape(-1, 128)


def per_device(covariates, intervals, offsets, responses, counts, smoothing):
    sums = local_sums(counts, covariates, intervals, offsets, responses)
    shares = sum_repeat(exchange(sums, NEAR, SHARES), SHARES, 16)
    shares = sum_repeat(exchange(shares, FAR, 16, FAR_GROUPS), 16, SHARES)
    factor, projected = factorize(exchange(shares, NEAR, SHARES), smoothing)
    return factor, projected[0]


def solution(mesh):
    fine = Mesh(mesh.devices.reshape(4, 2, 4, 2, 2, 4), ("zf", "zn", "yf", "yn", "core", "x"))
    spread = fine.axis_names
    return jax.shard_map(
        per_device,
        mesh=fine,
        in_specs=(P(None, spread), P(spread), P(spread), P(spread), P(spread), P()),
        out_specs=(P(), P()),
        check_vma=False,
    )
```
